512 devices in a mesh: rep: 8 (over z), kv: 64 (over x, y, core).
Axes of the slice: x: 4, y: 8, z: 8, core: 2. Of those that a mesh axis runs over, the one named last changes fastest.
Arguments:
- queries: bfloat16 [64, 64, 576], P('rep'), parts along dimension 0, may hold values from -400 to 400
- latent_cache: bfloat16 [64, 16384, 576], P('rep', 'kv'), parts along dimension 0, may hold values from -6.1 to 6.1
- lengths: int32 [64], P('rep'), parts along dimension 0, may hold values from 8192 to 16384, as said below
- value_up: bfloat16 [64, 512, 128], P('kv'), may hold values from -1 to 1
- out_proj: bfloat16 [8192, 7168], P('kv'), may hold values from -0.1875 to 0.1875
Outputs:
- attended: bfloat16 [64, 7168], P('rep', 'kv'), parts along dimension 0
The draws below stay inside these ranges and needn't reach their ends.
There are 8 independent parts, one for each index of `rep`. The reference program is written for one: setup_inputs(seed, part) draws one part's arguments, and reference() takes and returns one part's arrays. A program takes and returns all parts, laid end to end along the dimension named above; an argument that names none is the same for every part. Nothing has to cross between parts.
Inputs may be any that keep to these rules, and one draw needn't show every extreme that they name: `lengths`: some request has length 16384.
All inputs are finite; a program needn't handle non-finite values.
Results may differ from the reference program's by a relative error of at most 0.02.
Values sent between devices are 32-bit elements; how exact they have to be, the bound alone decides.
No kernel may reach another device: no remote copies, remote signals or barrier semaphores. Data moves between devices by JAX's collectives and lax.ppermute only.
A program may use at most 64 MiB of HBM per device.

```python
import jax
import jax.numpy as jnp
from jax import lax

ROWS = 8
S_DEV = 256
HEADS = 64
LATENT = 512
VDIM = 128
D = 7168
KDIM = 576
CTX = 16384
N_KV = 64


def shared_cache(key):
    normals = jax.random.normal(jax.random.fold_in(key, 11), (ROWS, CTX, KDIM), jnp.float32)
    return jnp.clip(normals, -6.0, 6.0)


def draw_latent_cache(key, part):
    base_key = key
    cache = shared_cache(base_key)
    return cache.astype(jnp.bfloat16)


def draw_queries(key, part):
    key = jax.random.fold_in(key, 5)
    normals = jnp.clip(jax.random.normal(key, (ROWS, HEADS, KDIM), jnp.float32), -6.0, 6.0) * 1.4
    return normals.astype(jnp.bfloat16)


def draw_lengths(key, part):
    key = jax.random.fold_in(key, 7)
    drawn = jax.random.randint(jax.random.fold_in(key, 1), (ROWS,), CTX // 2, CTX + 1)
    longest = jax.random.randint(jax.random.fold_in(key, 2), (), 0, ROWS)
    return drawn.at[longest].set(CTX).astype(jnp.int32)


def raised(array, rng, source, target, parts, factor):
    def block_of(dim):
        return (jnp.arange(array.shape[dim]) // (array.shape[dim] // parts)).reshape((-1,) + (1,) * (array.ndim - 1 - dim))

    near = jax.random.permutation(rng, parts)[block_of(target)]
    other_side = (block_of(target) + parts // 2) % parts
    return jnp.where((block_of(source) == near) | (block_of(source) == other_side), factor * array, array)


def block_scale(rng, extent, shards, smallest, high):
    factor_of, own = 1.0, jax.random.fold_in(rng, 6)
    for axis_at, blocks in shards:
        heights = jnp.exp(jax.random.uniform(jax.random.fold_in(own, axis_at), (blocks,), jnp.float32, smallest / len(shards), high / len(shards)))
        factor_of = factor_of * jnp.repeat(heights, extent[axis_at] // blocks).reshape([-1 if axis == axis_at else 1 for axis in range(len(extent))])
    return factor_of


def bell_draw(stream_key, shape, width, reach, pieces=(), held_as=jnp.bfloat16):
    gain = block_scale(stream_key, shape, pieces, -0.22, 0.18) if pieces else 1.0
    result = jax.random.normal(stream_key, shape, jnp.float32) * width * gain
    return jnp.minimum(jnp.maximum(result, -reach), reach).astype(held_as)


def gaussian_with(own_key, shape, width, most, split, heavy, kind=jnp.bfloat16):
    values = width * jax.random.normal(own_key, shape, jnp.float32)
    if split:
        values = values * block_scale(own_key, shape, split, -0.22, 0.18)
    return jnp.clip(raised(values, jax.random.fold_in(own_key, 3), *heavy), -most, most).astype(kind)


def setup_inputs(seed: int = 0, part: int = 0) -> dict:
    streams_of = jax.random.split(jax.random.key(seed), 6)
    own_keys = jax.random.split(jax.random.fold_in(streams_of[5], part), 6)
    return {
        "queries": draw_queries(jax.random.fold_in(jax.random.fold_in(streams_of[5], part), 71), part),
        "latent_cache": draw_latent_cache(jax.random.fold_in(jax.random.fold_in(streams_of[5], part), 71), part),
        "lengths": draw_lengths(jax.random.fold_in(jax.random.fold_in(streams_of[5], part), 71), part),
        "value_up": bell_draw(streams_of[3], (HEADS, LATENT, VDIM), (LATENT // 16) ** -0.5, 1.0, ((0, 64),)),
        "out_proj": gaussian_with(streams_of[4], (HEADS * VDIM, D), (HEADS * VDIM) ** -0.5, 0.1875, ((0, 64),), (0, 1, 64, 4.0)),
    }


softmax_scale = 192.0 ** -0.5
masked_value = -1e30


def reference(queries, latent_cache, lengths, value_up, out_proj):
    blocks = latent_cache.reshape(ROWS, N_KV, S_DEV, KDIM)
    query_wide = queries.astype(jnp.float32)

    def block_stats(block_index):
        cache_block = blocks[:, block_index].astype(jnp.float32)
        scores = jnp.einsum("rhk,rsk->rhs", query_wide, cache_block) * softmax_scale
        positions = block_index * S_DEV + jnp.arange(S_DEV, dtype=jnp.int32)
        live_mask = positions[None, :] < lengths[:, None]
        scores = jnp.where(live_mask[:, None, :], scores, masked_value)
        maxima = jnp.max(scores, axis=-1)
        exponents = jnp.where(live_mask[:, None, :], jnp.exp(scores - maxima[..., None]), 0.0)
        totals = jnp.sum(exponents, axis=-1)
        weights = exponents.astype(jnp.bfloat16).astype(jnp.float32)
        numerators = jnp.einsum("rhs,rsl->rhl", weights, cache_block[:, :, :LATENT])
        source_out = (numerators / jnp.maximum(totals, 1.0)[..., None]).astype(jnp.bfloat16)
        return source_out, maxima, totals

    source_out, source_max, source_sum = lax.map(block_stats, jnp.arange(N_KV, dtype=jnp.int32))
    global_max = jnp.max(source_max, axis=0)
    scaled = source_sum * jnp.exp(source_max - global_max[None])
    coefficient = scaled / jnp.sum(scaled, axis=0)[None]
    combined = jnp.sum(coefficient[..., None] * source_out.astype(jnp.float32), axis=0).astype(jnp.bfloat16)
    head_values = jnp.einsum("rhl,hlv->rhv", combined.astype(jnp.float32), value_up.astype(jnp.float32)).astype(jnp.bfloat16)
    flat_values = head_values.reshape(ROWS, HEADS * VDIM)
    return jnp.dot(flat_values, out_proj, preferred_element_type=jnp.float32).astype(jnp.bfloat16)
```

```python
import jax
import jax.numpy as jnp
from jax import lax
from jax.sharding import PartitionSpec as P

LATENT = 512


softmax_scale = 192.0 ** (-0.5)
masked_value = -1e30


def core_swap(x, kv):
    return lax.ppermute(x, "kv", [(i, i ^ 1) for i in range(kv)])


def merge_two(a, b):
    top = jnp.maximum(a[..., LATENT : LATENT + 1], b[..., LATENT : LATENT + 1])
    lane = lax.broadcasted_iota(jnp.int32, a.shape, a.ndim - 1)
    wa = jnp.where(lane == LATENT, 1.0, jnp.exp(a[..., LATENT : LATENT + 1] - top))
    wb = jnp.exp(b[..., LATENT : LATENT + 1] - top)
    return jnp.where(lane == LATENT, top, a * wa + b * wb)


def on_device(kv, queries, latent_cache, lengths, value_up, out_proj):
    rows, shard_len = latent_cache.shape[:2]
    heads = queries.shape[1]
    me = lax.axis_index("kv")
    core = lax.rem(me, 2)
    offset = me * shard_len
    positions = offset + jnp.arange(shard_len, dtype=jnp.int32)
    live_mask = positions[None, :] < lengths[:, None]
    scores = (
        jnp.einsum("rhk,rsk->rhs", queries, latent_cache, preferred_element_type=jnp.float32)
        * softmax_scale
    )
    scores = jnp.where(live_mask[:, None, :], scores, masked_value)
    maxima = jnp.max(scores, axis=-1)
    exponents = jnp.where(live_mask[:, None, :], jnp.exp(scores - maxima[..., None]), 0.0)
    totals = jnp.sum(exponents, axis=-1)
    numerators = jnp.einsum(
        "rhs,rsl->rhl",
        exponents.astype(jnp.bfloat16),
        latent_cache[:, :, :LATENT],
        preferred_element_type=jnp.float32,
    )
    stats = jnp.stack([maxima, totals], axis=-1)
    packed = jnp.concatenate([numerators, jnp.pad(stats, ((0, 0), (0, 0), (0, 126)))], axis=-1)
    packed = packed.reshape(rows, heads // 2, 2, LATENT + 128).transpose(2, 1, 0, 3)
    mine = lax.dynamic_index_in_dim(packed, core, 0, keepdims=False)
    theirs = lax.dynamic_index_in_dim(packed, 1 - core, 0, keepdims=False)
    pair = merge_two(mine, core_swap(theirs, kv))
    chips = [[2 * i + c for i in range(kv // 2)] for c in range(2)]
    got = lax.all_to_all(pair, "kv", 0, 0, axis_index_groups=chips)
    top = got[..., LATENT]
    weight = jnp.exp(top - jnp.max(top, axis=0)[None])
    total = jnp.sum(weight * got[..., LATENT + 1], axis=0)
    combined = jnp.sum(weight[..., None] * got[..., :LATENT], axis=0) / total[..., None]
    head_values = jnp.dot(
        combined.astype(jnp.bfloat16), value_up[0], preferred_element_type=jnp.float32
    )
    projection = jnp.dot(
        head_values.astype(jnp.bfloat16), out_proj, preferred_element_type=jnp.float32
    )
    features = out_proj.shape[1] // kv
    blocks = projection.reshape(rows, kv // 2, 2, features).transpose(2, 1, 0, 3)
    mine = lax.dynamic_index_in_dim(blocks, core, 0, keepdims=False)
    theirs = lax.dynamic_index_in_dim(blocks, 1 - core, 0, keepdims=False)
    summed = mine + core_swap(theirs, kv)
    parts = lax.all_to_all(summed, "kv", 0, 0, axis_index_groups=chips)
    return jnp.sum(parts, axis=0).astype(jnp.bfloat16)


def solution(mesh):
    kv = mesh.shape["kv"]
    placed = (
        P("rep", None, None),
        P("rep", "kv", None),
        P("rep"),
        P("kv", None, None),
        P("kv", None),
    )

    def device_step(*args):
        return on_device(kv, *args)

    return jax.shard_map(
        device_step, mesh=mesh, in_specs=placed, out_specs=P("rep", "kv"), check_vma=False
    )
```

```python
import jax
import jax.numpy as jnp
from jax import lax
from jax.experimental import pallas as pl
from jax.experimental.pallas import tpu as pltpu
from jax.sharding import PartitionSpec as P

LATENT = 512
LANES = 128
TILES = LATENT // LANES
HALF = LANES // 2

softmax_scale = 192.0 ** (-0.5)
masked_value = -1e30


def vmem_specs(n):
    return [pl.BlockSpec(memory_space=pltpu.VMEM)] * n


def in_hbm(x):
    return pltpu.with_memory_space_constraint(x, pltpu.HBM)


def lane_of(rows):
    return lax.broadcasted_iota(jnp.int32, (rows, LANES), 1)


def attend(lengths, queries, cache, theirs, mine, l_buf, q_buf, k_buf, s_buf, arrived):
    rows, heads, _ = queries.shape
    shard_len = cache.shape[2]
    pairs = heads // 2
    block = rows * (TILES + 1)
    me = lax.axis_index("kv")
    first_core = lax.rem(me, 2) == 0
    small = [
        pltpu.make_async_copy(lengths, l_buf, arrived.at[rows]),
        pltpu.make_async_copy(queries, q_buf, arrived.at[rows + 1]),
    ]
    large = [pltpu.make_async_copy(cache.at[r], k_buf.at[r], arrived.at[r]) for r in range(rows)]
    for copy in small + large:
        copy.start()
    position = me * shard_len + lax.broadcasted_iota(jnp.int32, (1, shard_len), 1)
    first_half = lane_of(pairs) < HALF
    live, weights, stats = {}, {}, {}

    def score(r):
        live[r] = position < l_buf[r]
        scores = jnp.dot(q_buf[r], k_buf[r], preferred_element_type=jnp.float32) * softmax_scale
        scores = jnp.where(live[r], scores, masked_value)
        for t in range(shard_len // LANES):
            s_buf[r, t] = scores[:, t * LANES : (t + 1) * LANES]

    def soften(r):
        exponents, packed = [], []
        for parity in range(2):
            part = jnp.concatenate(
                [s_buf[r, t, pl.ds(parity, pairs, stride=2), :] for t in range(shard_len // LANES)],
                axis=1,
            )
            top = jnp.max(part, axis=1, keepdims=True)
            exponent = jnp.where(live[r], jnp.exp(part - top), 0.0)
            exponents.append(exponent)
            packed.append(jnp.where(first_half, top, jnp.sum(exponent, axis=1, keepdims=True)))
        even, odd = exponents
        weights[r] = jnp.concatenate(
            [jnp.where(first_core, odd, even), jnp.where(first_core, even, odd)], axis=0
        ).astype(jnp.bfloat16)
        even, odd = packed
        stats[r] = jnp.where(first_core, odd, even), jnp.where(first_core, even, odd)

    def weigh(r):
        numerators = lax.dot_general(
            weights[r],
            k_buf[r, :LATENT, :],
            (((1,), (1,)), ((), ())),
            preferred_element_type=jnp.float32,
        )
        for k, out in enumerate((theirs, mine)):
            part = numerators[k * pairs : (k + 1) * pairs]
            for t in range(TILES):
                out[pl.ds(t * rows + r, pairs, stride=block), :] = part[:, t * LANES : (t + 1) * LANES]
            out[pl.ds(TILES * rows + r, pairs, stride=block), :] = stats[r][k]

    for copy in small:
        copy.wait()
    groups = 2
    size = rows // groups
    for step in range(groups + 2):
        if step < groups:
            for r in range(step * size, (step + 1) * size):
                large[r].wait()
        for group, stage in ((step - 2, weigh), (step - 1, soften), (step, score)):
            if 0 <= group < groups:
                for r in range(group * size, (group + 1) * size):
                    stage(r)


def merge_cores(rows, got, mine, merged):
    block = rows * (TILES + 1)
    sent = rows * TILES + 1
    lane = lane_of(rows)
    first_half = lane < HALF
    diagonal = lax.rem(lane, HALF) == lax.broadcasted_iota(jnp.int32, (rows, LANES), 0)
    for q in range(got.shape[0] // block):
        stats = [ref[q * block + rows * TILES : (q + 1) * block, :] for ref in (got, mine)]
        tops = [jnp.where(first_half, s, pltpu.roll(s, HALF, 1)) for s in stats]
        top = jnp.maximum(*tops)
        weights = [jnp.exp(t - top) for t in tops]
        for t in range(TILES):
            at = pl.ds(q * block + t * rows, rows)
            merged[q * sent + t * rows : q * sent + (t + 1) * rows, :] = (
                got[at, :] * weights[0] + mine[at, :] * weights[1]
            )
        both = jnp.where(first_half, top, stats[0] * weights[0] + stats[1] * weights[1])
        merged[q * sent + TILES * rows : (q + 1) * sent, :] = jnp.sum(
            jnp.where(diagonal, both, 0.0), axis=0, keepdims=True
        )


def project(rows, got, value_up, out_proj, theirs, mine):
    sent = rows * TILES + 1
    chips = got.shape[0] // sent
    features = out_proj.shape[1] // (2 * chips)
    core = lax.rem(lax.axis_index("kv"), 2)
    stats = got[pl.ds(TILES * rows, chips, stride=sent), :]
    weight = jnp.exp(stats - jnp.max(stats, axis=0, keepdims=True))
    total = jnp.sum(weight * pltpu.roll(stats, HALF, 1), axis=0, keepdims=True)
    coefficient = jnp.transpose(jnp.where(lane_of(chips) < rows, weight / total, 0.0))[:rows]
    combined = [jnp.zeros((rows, LANES), jnp.float32) for _ in range(TILES)]
    for j in range(chips):
        factor = jnp.broadcast_to(coefficient[:, j : j + 1], (rows, LANES))
        for t in range(TILES):
            combined[t] += factor * got[j * sent + t * rows : j * sent + (t + 1) * rows, :]
    head_values = jnp.dot(
        jnp.concatenate(combined, axis=1).astype(jnp.bfloat16),
        value_up[0],
        preferred_element_type=jnp.float32,
    )
    projection = jnp.dot(
        head_values.astype(jnp.bfloat16), out_proj[...], preferred_element_type=jnp.float32
    )
    pad = jnp.zeros((rows, LANES - features), jnp.float32)
    for q in range(chips):
        blocks = [
            jnp.concatenate([projection[:, d * features : (d + 1) * features], pad], axis=1)
            for d in (2 * q, 2 * q + 1)
        ]
        theirs[q] = jnp.where(core == 0, blocks[1], blocks[0])
        mine[q] = jnp.where(core == 0, blocks[0], blocks[1])


def core_swap(x, kv):
    return lax.ppermute(x, "kv", [(i, i ^ 1) for i in range(kv)])


def on_device(kv, queries, latent_cache, lengths, value_up, out_proj):
    rows, heads, width = queries.shape
    shard_len = latent_cache.shape[1]
    chips = kv // 2
    same_core = [[2 * i + c for i in range(chips)] for c in range(2)]
    params = pltpu.CompilerParams(vmem_limit_bytes=40 * 2**20)
    f32 = jnp.float32

    block = rows * (TILES + 1)
    sent = rows * TILES + 1
    partials = jax.ShapeDtypeStruct((chips * block, LANES), f32)
    theirs, mine = pl.pallas_call(
        attend,
        out_shape=[partials] * 2,
        in_specs=[pl.BlockSpec(memory_space=pltpu.HBM)] * 3,
        out_specs=vmem_specs(2),
        scratch_shapes=[
            pltpu.SMEM((rows,), lengths.dtype),
            pltpu.VMEM((rows, heads, width), queries.dtype),
            pltpu.VMEM((rows, width, shard_len), latent_cache.dtype),
            pltpu.VMEM((rows, shard_len // LANES, heads, LANES), f32),
            pltpu.SemaphoreType.DMA((rows + 2,)),
        ],
        compiler_params=params,
    )(*[in_hbm(v) for v in (lengths, queries, latent_cache.transpose(0, 2, 1))])
    got = core_swap(theirs, kv)
    merged = pl.pallas_call(
        lambda *refs: merge_cores(rows, *refs),
        out_shape=jax.ShapeDtypeStruct((chips * sent, LANES), f32),
        in_specs=vmem_specs(2),
        out_specs=vmem_specs(1)[0],
        compiler_params=params,
    )(got, mine)
    got = lax.all_to_all(
        merged.reshape(chips, 1, sent * LANES), "kv", 0, 0, axis_index_groups=same_core
    ).reshape(chips * sent, LANES)
    features = jax.ShapeDtypeStruct((chips, rows, LANES), f32)
    theirs, mine = pl.pallas_call(
        lambda *refs: project(rows, *refs),
        out_shape=[features] * 2,
        in_specs=vmem_specs(3),
        out_specs=vmem_specs(2),
        compiler_params=params,
    )(got, value_up, out_proj)
    summed = mine + core_swap(theirs, kv)
    parts = lax.all_to_all(summed, "kv", 0, 0, axis_index_groups=same_core)
    return jnp.sum(parts, axis=0)[:, : out_proj.shape[1] // kv].astype(jnp.bfloat16)


def solution(mesh):
    kv = mesh.shape["kv"]
    placed = (
        P("rep", None, None),
        P("rep", "kv", None),
        P("rep"),
        P("kv", None, None),
        P("kv", None),
    )

    def device_step(*args):
        return on_device(kv, *args)

    return jax.shard_map(
        device_step, mesh=mesh, in_specs=placed, out_specs=P("rep", "kv"), check_vma=False
    )
```

```python
import jax
import jax.numpy as jnp
from jax import lax
from jax.experimental import pallas as pl
from jax.experimental.pallas import tpu as pltpu
from jax.sharding import PartitionSpec as P

LATENT = 512
LANES = 128
TILES = LATENT // LANES
HALF = LANES // 2

softmax_scale = 192.0 ** (-0.5)
masked_value = -1e30


def vmem_specs(n):
    return [pl.BlockSpec(memory_space=pltpu.VMEM)] * n


def in_hbm(x):
    return pltpu.with_memory_space_constraint(x, pltpu.HBM)


def lane_of(rows):
    return lax.broadcasted_iota(jnp.int32, (rows, LANES), 1)


def soften(s_buf, r, parity):
    pairs = s_buf.shape[2] // 2
    part = jnp.concatenate(
        [s_buf[r, t, pl.ds(parity, pairs, stride=2), :] for t in range(s_buf.shape[1])], axis=1
    )
    top = jnp.max(part, axis=1, keepdims=True)
    exponent = jnp.where(part > 0.5 * masked_value, jnp.exp(part - top), 0.0)
    packed = jnp.where(lane_of(pairs) < HALF, top, jnp.sum(exponent, axis=1, keepdims=True))
    return exponent, packed


def soften_one(s_buf, r, odd_wanted):
    even, odd = soften(s_buf, r, 0), soften(s_buf, r, 1)
    exponent, packed = [jnp.where(odd_wanted, b, a) for a, b in zip(even, odd)]
    return exponent.astype(jnp.bfloat16), packed


def weigh(out, weights, packed, k_buf, r):
    rows = k_buf.shape[0]
    pairs = weights.shape[0]
    block = rows * (TILES + 1)
    numerators = lax.dot_general(
        weights, k_buf[r, :LATENT, :], (((1,), (1,)), ((), ())), preferred_element_type=jnp.float32
    )
    for t in range(TILES):
        out[pl.ds(t * rows + r, pairs, stride=block), :] = numerators[:, t * LANES : (t + 1) * LANES]
    out[pl.ds(TILES * rows + r, pairs, stride=block), :] = packed


def attend_theirs(lengths, queries, cache, theirs, s_buf, k_buf, l_buf, q_buf, arrived):
    rows = queries.shape[0]
    shard_len = cache.shape[2]
    me = lax.axis_index("kv")
    first_core = lax.rem(me, 2) == 0
    small = [
        pltpu.make_async_copy(lengths, l_buf, arrived.at[rows]),
        pltpu.make_async_copy(queries, q_buf, arrived.at[rows + 1]),
    ]
    large = [pltpu.make_async_copy(cache.at[r], k_buf.at[r], arrived.at[r]) for r in range(rows)]
    for copy in small + large:
        copy.start()
    position = me * shard_len + lax.broadcasted_iota(jnp.int32, (1, shard_len), 1)
    softened = {}

    def score(r):
        scores = jnp.dot(q_buf[r], k_buf[r], preferred_element_type=jnp.float32) * softmax_scale
        scores = jnp.where(position < l_buf[r], scores, masked_value)
        for t in range(shard_len // LANES):
            s_buf[r, t] = scores[:, t * LANES : (t + 1) * LANES]

    def weights_of(r):
        softened[r] = soften_one(s_buf, r, first_core)

    def finish(r):
        weigh(theirs, *softened[r], k_buf, r)

    for copy in small:
        copy.wait()
    groups = 2
    size = rows // groups
    for step in range(groups + 2):
        if step < groups:
            for r in range(step * size, (step + 1) * size):
                large[r].wait()
        for group, stage in ((step - 2, finish), (step - 1, weights_of), (step, score)):
            if 0 <= group < groups:
                for r in range(group * size, (group + 1) * size):
                    stage(r)


def attend_mine(s_buf, k_buf, mine):
    first_core = lax.rem(lax.axis_index("kv"), 2) == 0
    softened = [soften_one(s_buf, r, jnp.logical_not(first_core)) for r in range(k_buf.shape[0])]
    for r, pair in enumerate(softened):
        weigh(mine, *pair, k_buf, r)


def merge_cores(rows, got, mine, merged):
    block = rows * (TILES + 1)
    sent = rows * TILES + 1
    lane = lane_of(rows)
    first_half = lane < HALF
    diagonal = lax.rem(lane, HALF) == lax.broadcasted_iota(jnp.int32, (rows, LANES), 0)
    for q in range(got.shape[0] // block):
        stats = [ref[q * block + rows * TILES : (q + 1) * block, :] for ref in (got, mine)]
        tops = [jnp.where(first_half, s, pltpu.roll(s, HALF, 1)) for s in stats]
        top = jnp.maximum(*tops)
        weights = [jnp.exp(t - top) for t in tops]
        for t in range(TILES):
            at = pl.ds(q * block + t * rows, rows)
            merged[q * sent + t * rows : q * sent + (t + 1) * rows, :] = (
                got[at, :] * weights[0] + mine[at, :] * weights[1]
            )
        both = jnp.where(first_half, top, stats[0] * weights[0] + stats[1] * weights[1])
        merged[q * sent + TILES * rows : (q + 1) * sent, :] = jnp.sum(
            jnp.where(diagonal, both, 0.0), axis=0, keepdims=True
        )


def project(rows, got, value_up, out_proj, theirs, mine):
    sent = rows * TILES + 1
    chips = got.shape[0] // sent
    features = out_proj.shape[1] // (2 * chips)
    core = lax.rem(lax.axis_index("kv"), 2)
    stats = got[pl.ds(TILES * rows, chips, stride=sent), :]
    weight = jnp.exp(stats - jnp.max(stats, axis=0, keepdims=True))
    total = jnp.sum(weight * pltpu.roll(stats, HALF, 1), axis=0, keepdims=True)
    coefficient = jnp.transpose(jnp.where(lane_of(chips) < rows, weight / total, 0.0))[:rows]
    combined = [jnp.zeros((rows, LANES), jnp.float32) for _ in range(TILES)]
    for j in range(chips):
        factor = jnp.broadcast_to(coefficient[:, j : j + 1], (rows, LANES))
        for t in range(TILES):
            combined[t] += factor * got[j * sent + t * rows : j * sent + (t + 1) * rows, :]
    head_values = jnp.dot(
        jnp.concatenate(combined, axis=1).astype(jnp.bfloat16),
        value_up[0],
        preferred_element_type=jnp.float32,
    )
    projection = jnp.dot(
        head_values.astype(jnp.bfloat16), out_proj[...], preferred_element_type=jnp.float32
    )
    spare = LANES - features
    lane = lane_of(rows)
    pad = jnp.zeros((rows, spare), jnp.float32)
    for q in range(chips):
        blocks = []
        for d in (2 * q, 2 * q + 1):
            part = jnp.concatenate([projection[:, d * features : (d + 1) * features], pad], axis=1)
            last = jnp.broadcast_to(part[rows - 1 :], (rows, LANES))
            last = pltpu.roll(last, spare, 1, stride=spare, stride_axis=0)
            blocks.append(jnp.where(lane < features, part, last))
        at = pl.ds(q * (rows - 1), rows - 1)
        theirs[at, :] = jnp.where(core == 0, blocks[1], blocks[0])[: rows - 1]
        mine[at, :] = jnp.where(core == 0, blocks[0], blocks[1])[: rows - 1]


def add_other(both, mine, out):
    out[...] = mine[...] + both[1 - lax.rem(lax.axis_index("kv"), 2)]


def add_up(got, out):
    rows, features = out.shape
    spare = LANES - features
    total = got[pl.ds(0, rows - 1), :]
    for j in range(1, got.shape[0] // (rows - 1)):
        total += got[pl.ds(j * (rows - 1), rows - 1), :]
    last = [total[i : i + 1, features:] for i in reversed(range(rows - 1))]
    out[...] = jnp.concatenate(
        [total[:, :features], jnp.concatenate(last, axis=1)], axis=0
    ).astype(out.dtype)


def core_swap(x, kv):
    return lax.ppermute(x, "kv", [(i, i ^ 1) for i in range(kv)])


def on_device(kv, queries, latent_cache, lengths, value_up, out_proj):
    rows, heads, width = queries.shape
    shard_len = latent_cache.shape[1]
    chips = kv // 2
    same_core = [[2 * i + c for i in range(chips)] for c in range(2)]
    params = pltpu.CompilerParams(vmem_limit_bytes=8 * 2**20)
    f32 = jnp.float32

    block = rows * (TILES + 1)
    sent = rows * TILES + 1
    partials = jax.ShapeDtypeStruct((chips * block, LANES), f32)
    theirs, scores, held = pl.pallas_call(
        attend_theirs,
        out_shape=[
            partials,
            jax.ShapeDtypeStruct((rows, shard_len // LANES, heads, LANES), f32),
            jax.ShapeDtypeStruct((rows, width, shard_len), latent_cache.dtype),
        ],
        in_specs=[pl.BlockSpec(memory_space=pltpu.HBM)] * 3,
        out_specs=vmem_specs(3),
        scratch_shapes=[
            pltpu.SMEM((rows,), lengths.dtype),
            pltpu.VMEM((rows, heads, width), queries.dtype),
            pltpu.SemaphoreType.DMA((rows + 2,)),
        ],
        compiler_params=params,
    )(*[in_hbm(v) for v in (lengths, queries, latent_cache.transpose(0, 2, 1))])
    got = core_swap(theirs, kv)
    mine = pl.pallas_call(
        attend_mine,
        out_shape=partials,
        in_specs=vmem_specs(2),
        out_specs=vmem_specs(1)[0],
        compiler_params=params,
    )(scores, held)
    merged = pl.pallas_call(
        lambda *refs: merge_cores(rows, *refs),
        out_shape=jax.ShapeDtypeStruct((chips * sent, LANES), f32),
        in_specs=vmem_specs(2),
        out_specs=vmem_specs(1)[0],
        compiler_params=params,
    )(got, mine)
    got = lax.all_to_all(
        merged.reshape(chips, 1, sent * LANES), "kv", 0, 0, axis_index_groups=same_core
    ).reshape(chips * sent, LANES)
    features = jax.ShapeDtypeStruct((chips * (rows - 1), LANES), f32)
    theirs, mine = pl.pallas_call(
        lambda *refs: project(rows, *refs),
        out_shape=[features] * 2,
        in_specs=vmem_specs(3),
        out_specs=vmem_specs(2),
        compiler_params=params,
    )(got, value_up, out_proj)
    both = lax.all_gather(
        theirs, "kv", axis_index_groups=[[2 * i, 2 * i + 1] for i in range(chips)]
    )
    summed = pl.pallas_call(
        add_other,
        out_shape=features,
        in_specs=vmem_specs(2),
        out_specs=vmem_specs(1)[0],
        compiler_params=params,
    )(both, mine)
    parts = lax.all_to_all(
        summed.reshape(chips, 1, (rows - 1) * LANES), "kv", 0, 0, axis_index_groups=same_core
    ).reshape(chips * (rows - 1), LANES)
    return pl.pallas_call(
        add_up,
        out_shape=jax.ShapeDtypeStruct((rows, out_proj.shape[1] // kv), jnp.bfloat16),
        in_specs=vmem_specs(1),
        compiler_params=params,
    )(parts)


def solution(mesh):
    kv = mesh.shape["kv"]
    placed = (
        P("rep", None, None),
        P("rep", "kv", None),
        P("rep"),
        P("kv", None, None),
        P("kv", None),
    )

    def device_step(*args):
        return on_device(kv, *args)

    return jax.shard_map(
        device_step, mesh=mesh, in_specs=placed, out_specs=P("rep", "kv"), check_vma=False
    )
```

```python
import jax
import jax.numpy as jnp
from jax import lax
from jax.experimental import pallas as pl
from jax.experimental.pallas import tpu as pltpu
from jax.sharding import PartitionSpec as P

LATENT = 512
LANES = 128
TILES = LATENT // LANES
HALF = LANES // 2

softmax_scale = 192.0 ** (-0.5)
masked_value = -1e30


def vmem_specs(n):
    return [pl.BlockSpec(memory_space=pltpu.VMEM)] * n


def in_hbm(x):
    return pltpu.with_memory_space_constraint(x, pltpu.HBM)


def lane_of(rows):
    return lax.broadcasted_iota(jnp.int32, (rows, LANES), 1)


def soften(s_buf, r, parity):
    pairs = s_buf.shape[2] // 2
    part = jnp.concatenate(
        [s_buf[r, t, pl.ds(parity, pairs, stride=2), :] for t in range(s_buf.shape[1])], axis=1
    )
    top = jnp.max(part, axis=1, keepdims=True)
    exponent = jnp.where(part > 0.5 * masked_value, jnp.exp(part - top), 0.0)
    packed = jnp.where(lane_of(pairs) < HALF, top, jnp.sum(exponent, axis=1, keepdims=True))
    return exponent, packed


def soften_one(s_buf, r, odd_wanted):
    even, odd = soften(s_buf, r, 0), soften(s_buf, r, 1)
    exponent, packed = [jnp.where(odd_wanted, b, a) for a, b in zip(even, odd)]
    return exponent.astype(jnp.bfloat16), packed


def weigh(out, weights, packed, k_buf, r):
    rows = k_buf.shape[0]
    pairs = weights.shape[0]
    block = rows * (TILES + 1)
    numerators = lax.dot_general(
        weights, k_buf[r, :LATENT, :], (((1,), (1,)), ((), ())), preferred_element_type=jnp.float32
    )
    for t in range(TILES):
        out[pl.ds(t * rows + r, pairs, stride=block), :] = numerators[:, t * LANES : (t + 1) * LANES]
    out[pl.ds(TILES * rows + r, pairs, stride=block), :] = packed


def attend_theirs(lengths, queries, cache, theirs, s_buf, k_buf, l_buf, q_buf, arrived):
    rows = queries.shape[0]
    shard_len = cache.shape[2]
    me = lax.axis_index("kv")
    first_core = lax.rem(me, 2) == 0
    small = [
        pltpu.make_async_copy(lengths, l_buf, arrived.at[rows]),
        pltpu.make_async_copy(queries, q_buf, arrived.at[rows + 1]),
    ]
    large = [pltpu.make_async_copy(cache.at[r], k_buf.at[r], arrived.at[r]) for r in range(rows)]
    for copy in small + large:
        copy.start()
    position = me * shard_len + lax.broadcasted_iota(jnp.int32, (1, shard_len), 1)
    softened = {}

    def score(r):
        scores = jnp.dot(q_buf[r], k_buf[r], preferred_element_type=jnp.float32) * softmax_scale
        scores = jnp.where(position < l_buf[r], scores, masked_value)
        for t in range(shard_len // LANES):
            s_buf[r, t] = scores[:, t * LANES : (t + 1) * LANES]

    def weights_of(r):
        softened[r] = soften_one(s_buf, r, first_core)

    def finish(r):
        weigh(theirs, *softened[r], k_buf, r)

    for copy in small:
        copy.wait()
    for copy in large:
        copy.wait()
    for stage in (score, weights_of, finish):
        for r in range(rows):
            stage(r)


def attend_mine(s_buf, k_buf, mine):
    first_core = lax.rem(lax.axis_index("kv"), 2) == 0
    softened = [soften_one(s_buf, r, jnp.logical_not(first_core)) for r in range(k_buf.shape[0])]
    for r, pair in enumerate(softened):
        weigh(mine, *pair, k_buf, r)


def merge_cores(rows, order, got, mine, merged):
    block = rows * (TILES + 1)
    sent = rows * TILES + 1
    lane = lane_of(rows)
    first_half = lane < HALF
    diagonal = lax.rem(lane, HALF) == lax.broadcasted_iota(jnp.int32, (rows, LANES), 0)
    for slot, q in enumerate(order):
        stats = [ref[q * block + rows * TILES : (q + 1) * block, :] for ref in (got, mine)]
        tops = [jnp.where(first_half, s, pltpu.roll(s, HALF, 1)) for s in stats]
        top = jnp.maximum(*tops)
        weights = [jnp.exp(t - top) for t in tops]
        for t in range(TILES):
            at = pl.ds(q * block + t * rows, rows)
            merged[slot * sent + t * rows : slot * sent + (t + 1) * rows, :] = (
                got[at, :] * weights[0] + mine[at, :] * weights[1]
            )
        both = jnp.where(first_half, top, stats[0] * weights[0] + stats[1] * weights[1])
        merged[slot * sent + TILES * rows : (slot + 1) * sent, :] = jnp.sum(
            jnp.where(diagonal, both, 0.0), axis=0, keepdims=True
        )


def project(rows, order, got, value_up, out_proj, theirs, mine):
    sent = rows * TILES + 1
    chips = got.shape[0] // sent
    features = out_proj.shape[1] // (2 * chips)
    core = lax.rem(lax.axis_index("kv"), 2)
    stats = got[pl.ds(TILES * rows, chips, stride=sent), :]
    weight = jnp.exp(stats - jnp.max(stats, axis=0, keepdims=True))
    total = jnp.sum(weight * pltpu.roll(stats, HALF, 1), axis=0, keepdims=True)
    coefficient = jnp.transpose(jnp.where(lane_of(chips) < rows, weight / total, 0.0))[:rows]
    combined = [jnp.zeros((rows, LANES), jnp.float32) for _ in range(TILES)]
    for j in range(chips):
        factor = jnp.broadcast_to(coefficient[:, j : j + 1], (rows, LANES))
        for t in range(TILES):
            combined[t] += factor * got[j * sent + t * rows : j * sent + (t + 1) * rows, :]
    head_values = jnp.dot(
        jnp.concatenate(combined, axis=1).astype(jnp.bfloat16),
        value_up[0],
        preferred_element_type=jnp.float32,
    )
    projection = jnp.dot(
        head_values.astype(jnp.bfloat16), out_proj[...], preferred_element_type=jnp.float32
    )
    spare = LANES - features
    lane = lane_of(rows)
    pad = jnp.zeros((rows, spare), jnp.float32)
    for slot, q in enumerate(order):
        blocks = []
        for d in (2 * q, 2 * q + 1):
            part = jnp.concatenate([projection[:, d * features : (d + 1) * features], pad], axis=1)
            last = jnp.broadcast_to(part[rows - 1 :], (rows, LANES))
            last = pltpu.roll(last, spare, 1, stride=spare, stride_axis=0)
            blocks.append(jnp.where(lane < features, part, last))
        at = pl.ds(slot * (rows - 1), rows - 1)
        theirs[at, :] = jnp.where(core == 0, blocks[1], blocks[0])[: rows - 1]
        mine[at, :] = jnp.where(core == 0, blocks[0], blocks[1])[: rows - 1]


def add_other(both, mine, out):
    out[...] = mine[...] + both[1 - lax.rem(lax.axis_index("kv"), 2)]


def add_up(got, out):
    rows, features = out.shape
    spare = LANES - features
    total = got[pl.ds(0, rows - 1), :]
    for j in range(1, got.shape[0] // (rows - 1)):
        total += got[pl.ds(j * (rows - 1), rows - 1), :]
    last = [total[i : i + 1, features:] for i in reversed(range(rows - 1))]
    out[...] = jnp.concatenate(
        [total[:, :features], jnp.concatenate(last, axis=1)], axis=0
    ).astype(out.dtype)


def core_swap(x, kv):
    return lax.ppermute(x, "kv", [(i, i ^ 1) for i in range(kv)])


def chip_order(chips):
    first = 19 % chips
    return [(first + i) % chips for i in range(chips)]


def on_device(kv, queries, latent_cache, lengths, value_up, out_proj):
    rows, heads, width = queries.shape
    shard_len = latent_cache.shape[1]
    chips = kv // 2
    order = chip_order(chips)
    same_core = [[2 * i + c for i in order] for c in range(2)]
    params = pltpu.CompilerParams(vmem_limit_bytes=8 * 2**20)
    f32 = jnp.float32

    block = rows * (TILES + 1)
    sent = rows * TILES + 1
    partials = jax.ShapeDtypeStruct((chips * block, LANES), f32)
    theirs, scores, held = pl.pallas_call(
        attend_theirs,
        out_shape=[
            partials,
            jax.ShapeDtypeStruct((rows, shard_len // LANES, heads, LANES), f32),
            jax.ShapeDtypeStruct((rows, width, shard_len), latent_cache.dtype),
        ],
        in_specs=[pl.BlockSpec(memory_space=pltpu.HBM)] * 3,
        out_specs=vmem_specs(3),
        scratch_shapes=[
            pltpu.SMEM((rows,), lengths.dtype),
            pltpu.VMEM((rows, heads, width), queries.dtype),
            pltpu.SemaphoreType.DMA((rows + 2,)),
        ],
        compiler_params=params,
    )(*[in_hbm(v) for v in (lengths, queries, latent_cache.transpose(0, 2, 1))])
    got = core_swap(theirs, kv)
    mine = pl.pallas_call(
        attend_mine,
        out_shape=partials,
        in_specs=vmem_specs(2),
        out_specs=vmem_specs(1)[0],
        compiler_params=params,
    )(scores, held)
    merged = pl.pallas_call(
        lambda *refs: merge_cores(rows, order, *refs),
        out_shape=jax.ShapeDtypeStruct((chips * sent, LANES), f32),
        in_specs=vmem_specs(2),
        out_specs=vmem_specs(1)[0],
        compiler_params=params,
    )(got, mine)
    got = lax.all_to_all(
        merged.reshape(chips, 1, sent * LANES), "kv", 0, 0, axis_index_groups=same_core
    ).reshape(chips * sent, LANES)
    features = jax.ShapeDtypeStruct((chips * (rows - 1), LANES), f32)
    theirs, mine = pl.pallas_call(
        lambda *refs: project(rows, order, *refs),
        out_shape=[features] * 2,
        in_specs=vmem_specs(3),
        out_specs=vmem_specs(2),
        compiler_params=params,
    )(got, value_up, out_proj)
    both = lax.all_gather(
        theirs, "kv", axis_index_groups=[[2 * i, 2 * i + 1] for i in range(chips)]
    )
    summed = pl.pallas_call(
        add_other,
        out_shape=features,
        in_specs=vmem_specs(2),
        out_specs=vmem_specs(1)[0],
        compiler_params=params,
    )(both, mine)
    parts = lax.all_to_all(
        summed.reshape(chips, 1, (rows - 1) * LANES), "kv", 0, 0, axis_index_groups=same_core
    ).reshape(chips * (rows - 1), LANES)
    return pl.pallas_call(
        add_up,
        out_shape=jax.ShapeDtypeStruct((rows, out_proj.shape[1] // kv), jnp.bfloat16),
        in_specs=vmem_specs(1),
        compiler_params=params,
    )(parts)


def solution(mesh):
    kv = mesh.shape["kv"]
    placed = (
        P("rep", None, None),
        P("rep", "kv", None),
        P("rep"),
        P("kv", None, None),
        P("kv", None),
    )

    def device_step(*args):
        return on_device(kv, *args)

    return jax.shard_map(
        device_step, mesh=mesh, in_specs=placed, out_specs=P("rep", "kv"), check_vma=False
    )
```

```python
import jax
import jax.numpy as jnp
from jax import lax
from jax.experimental import pallas as pl
from jax.experimental.pallas import tpu as pltpu
from jax.sharding import PartitionSpec as P

LATENT = 512
LANES = 128
TILES = LATENT // LANES
HALF = LANES // 2

softmax_scale = 192.0 ** (-0.5)
masked_value = -1e30


def vmem_specs(n):
    return [pl.BlockSpec(memory_space=pltpu.VMEM)] * n


def in_hbm(x):
    return pltpu.with_memory_space_constraint(x, pltpu.HBM)


def lane_of(rows):
    return lax.broadcasted_iota(jnp.int32, (rows, LANES), 1)


def soften(s_buf, r, odd_wanted, stats):
    pairs = s_buf.shape[2] // 2
    even, odd = [
        jnp.concatenate(
            [s_buf[r, t, pl.ds(parity, pairs, stride=2), :] for t in range(s_buf.shape[1])], axis=1
        )
        for parity in range(2)
    ]
    part = jnp.where(odd_wanted, odd, even)
    top = jnp.max(part, axis=1, keepdims=True)
    exponent = jnp.where(part > 0.5 * masked_value, jnp.exp(part - top), 0.0)
    lane = lane_of(pairs)
    stats = jnp.where(lane == r, top, stats)
    stats = jnp.where(lane == HALF + r, jnp.sum(exponent, axis=1, keepdims=True), stats)
    return exponent.astype(jnp.bfloat16), stats


def weigh(out, weights, k_buf, r):
    rows = k_buf.shape[0]
    pairs = weights.shape[0]
    numerators = lax.dot_general(
        weights, k_buf[r, :LATENT, :], (((1,), (1,)), ((), ())), preferred_element_type=jnp.float32
    )
    for t in range(TILES):
        out[pl.ds(t * rows + r, pairs, stride=rows * TILES + 1), :] = numerators[
            :, t * LANES : (t + 1) * LANES
        ]


def finish(out, s_buf, k_buf, odd_wanted):
    rows = k_buf.shape[0]
    pairs = s_buf.shape[2] // 2
    stats = jnp.zeros((pairs, LANES), jnp.float32)
    weights = []
    for r in range(rows):
        exponent, stats = soften(s_buf, r, odd_wanted, stats)
        weights.append(exponent)
    for r in range(rows):
        weigh(out, weights[r], k_buf, r)
    out[pl.ds(rows * TILES, pairs, stride=rows * TILES + 1), :] = stats


def attend_theirs(lengths, queries, cache, theirs, s_buf, k_buf, l_buf, q_buf, arrived):
    rows, heads, _ = queries.shape
    shard_len = cache.shape[2]
    me = lax.axis_index("kv")
    first_core = lax.rem(me, 2) == 0
    small = [
        pltpu.make_async_copy(lengths, l_buf, arrived.at[rows]),
        pltpu.make_async_copy(queries, q_buf, arrived.at[rows + 1]),
    ]
    large = [pltpu.make_async_copy(cache.at[r], k_buf.at[r], arrived.at[r]) for r in range(rows)]
    for copy in small + large:
        copy.start()
    position = me * shard_len + lax.broadcasted_iota(jnp.int32, (1, shard_len), 1)
    stats = [jnp.zeros((heads // 2, LANES), jnp.float32)]
    weights = {}

    def score(r):
        scores = jnp.dot(q_buf[r], k_buf[r], preferred_element_type=jnp.float32) * softmax_scale
        scores = jnp.where(position < l_buf[r], scores, masked_value)
        for t in range(shard_len // LANES):
            s_buf[r, t] = scores[:, t * LANES : (t + 1) * LANES]

    def exponents(r):
        weights[r], stats[0] = soften(s_buf, r, first_core, stats[0])

    def numerators(r):
        weigh(theirs, weights[r], k_buf, r)

    for copy in small:
        copy.wait()
    parts = [range(4), range(4, rows)]
    for step in range(4):
        if step < 2:
            for r in parts[step]:
                large[r].wait()
        for part, stage in ((step - 2, numerators), (step - 1, exponents), (step, score)):
            if 0 <= part < 2:
                for r in parts[part]:
                    stage(r)
    theirs[pl.ds(rows * TILES, heads // 2, stride=rows * TILES + 1), :] = stats[0]


def attend_mine(s_buf, k_buf, mine):
    finish(mine, s_buf, k_buf, lax.rem(lax.axis_index("kv"), 2) == 1)


def merge_cores(rows, order, got, mine, merged):
    sent = rows * TILES + 1
    chips = len(order)
    stats = [ref[pl.ds(rows * TILES, chips, stride=sent), :] for ref in (got, mine)]
    top = jnp.maximum(*stats)
    weights = [jnp.exp(s - top) for s in stats]
    total = sum(pltpu.roll(s, HALF, 1) * w for s, w in zip(stats, weights))
    both = jnp.where(lane_of(chips) < HALF, top, pltpu.roll(total, HALF, 1))
    columns = [jnp.transpose(w)[:rows] for w in weights]
    for slot, q in enumerate(order):
        factors = [jnp.broadcast_to(c[:, q : q + 1], (rows, LANES)) for c in columns]
        for t in range(TILES):
            at = pl.ds(q * sent + t * rows, rows)
            merged[slot * sent + t * rows : slot * sent + (t + 1) * rows, :] = (
                got[at, :] * factors[0] + mine[at, :] * factors[1]
            )
        merged[slot * sent + TILES * rows : (slot + 1) * sent, :] = both[q : q + 1]


def project(rows, order, got, value_up, out_proj, theirs, mine):
    sent = rows * TILES + 1
    chips = got.shape[0] // sent
    features = out_proj.shape[1] // (2 * chips)
    core = lax.rem(lax.axis_index("kv"), 2)
    stats = got[pl.ds(TILES * rows, chips, stride=sent), :]
    weight = jnp.exp(stats - jnp.max(stats, axis=0, keepdims=True))
    column = jnp.transpose(weight)[:rows]
    total = jnp.sum(
        jnp.transpose(weight * pltpu.roll(stats, HALF, 1))[:rows], axis=1, keepdims=True
    )
    combined = [jnp.zeros((rows, LANES), jnp.float32) for _ in range(TILES)]
    for j in range(chips):
        factor = jnp.broadcast_to(column[:, j : j + 1], (rows, LANES))
        for t in range(TILES):
            combined[t] += factor * got[j * sent + t * rows : j * sent + (t + 1) * rows, :]
    head_values = jnp.dot(
        jnp.concatenate(combined, axis=1).astype(jnp.bfloat16),
        value_up[0],
        preferred_element_type=jnp.float32,
    )
    projection = jnp.dot(
        (head_values / total).astype(jnp.bfloat16), out_proj[...], preferred_element_type=jnp.float32
    )
    spare = LANES - features
    lane = lane_of(rows)
    pad = jnp.zeros((rows, spare), jnp.float32)
    for slot, q in enumerate(order):
        blocks = []
        for d in (2 * q, 2 * q + 1):
            part = jnp.concatenate([projection[:, d * features : (d + 1) * features], pad], axis=1)
            last = jnp.broadcast_to(part[rows - 1 :], (rows, LANES))
            last = pltpu.roll(last, spare, 1, stride=spare, stride_axis=0)
            blocks.append(jnp.where(lane < features, part, last))
        at = pl.ds(slot * (rows - 1), rows - 1)
        theirs[at, :] = jnp.where(core == 0, blocks[1], blocks[0])[: rows - 1]
        mine[at, :] = jnp.where(core == 0, blocks[0], blocks[1])[: rows - 1]


def add_other(both, mine, out):
    out[...] = mine[...] + both[1 - lax.rem(lax.axis_index("kv"), 2)]


def add_up(got, out):
    rows, features = out.shape
    spare = LANES - features
    total = got[pl.ds(0, rows - 1), :]
    for j in range(1, got.shape[0] // (rows - 1)):
        total += got[pl.ds(j * (rows - 1), rows - 1), :]
    last = [total[i : i + 1, features:] for i in reversed(range(rows - 1))]
    out[...] = jnp.concatenate(
        [total[:, :features], jnp.concatenate(last, axis=1)], axis=0
    ).astype(out.dtype)


def core_swap(x, kv):
    return lax.ppermute(x, "kv", [(i, i ^ 1) for i in range(kv)])


def chip_order(chips):
    first = 19 % chips
    return [(first + i) % chips for i in range(chips)]


def on_device(kv, queries, latent_cache, lengths, value_up, out_proj):
    rows, heads, width = queries.shape
    shard_len = latent_cache.shape[1]
    chips = kv // 2
    order = chip_order(chips)
    same_core = [[2 * i + c for i in order] for c in range(2)]
    params = pltpu.CompilerParams(vmem_limit_bytes=8 * 2**20)
    f32 = jnp.float32

    sent = rows * TILES + 1
    partials = jax.ShapeDtypeStruct((chips * sent, LANES), f32)
    theirs, scores, held = pl.pallas_call(
        attend_theirs,
        out_shape=[
            partials,
            jax.ShapeDtypeStruct((rows, shard_len // LANES, heads, LANES), f32),
            jax.ShapeDtypeStruct((rows, width, shard_len), latent_cache.dtype),
        ],
        in_specs=[pl.BlockSpec(memory_space=pltpu.HBM)] * 3,
        out_specs=vmem_specs(3),
        scratch_shapes=[
            pltpu.SMEM((rows,), lengths.dtype),
            pltpu.VMEM((rows, heads, width), queries.dtype),
            pltpu.SemaphoreType.DMA((rows + 2,)),
        ],
        compiler_params=params,
    )(*[in_hbm(v) for v in (lengths, queries, latent_cache.transpose(0, 2, 1))])
    got = core_swap(theirs, kv)
    mine = pl.pallas_call(
        attend_mine,
        out_shape=partials,
        in_specs=vmem_specs(2),
        out_specs=vmem_specs(1)[0],
        compiler_params=params,
    )(scores, held)
    merged = pl.pallas_call(
        lambda *refs: merge_cores(rows, order, *refs),
        out_shape=partials,
        in_specs=vmem_specs(2),
        out_specs=vmem_specs(1)[0],
        compiler_params=params,
    )(got, mine)
    got = lax.all_to_all(
        merged.reshape(chips, 1, sent * LANES), "kv", 0, 0, axis_index_groups=same_core
    ).reshape(chips * sent, LANES)
    features = jax.ShapeDtypeStruct((chips * (rows - 1), LANES), f32)
    theirs, mine = pl.pallas_call(
        lambda *refs: project(rows, order, *refs),
        out_shape=[features] * 2,
        in_specs=vmem_specs(3),
        out_specs=vmem_specs(2),
        compiler_params=params,
    )(got, value_up, out_proj)
    both = lax.all_gather(
        theirs, "kv", axis_index_groups=[[2 * i, 2 * i + 1] for i in range(chips)]
    )
    summed = pl.pallas_call(
        add_other,
        out_shape=features,
        in_specs=vmem_specs(2),
        out_specs=vmem_specs(1)[0],
        compiler_params=params,
    )(both, mine)
    parts = lax.all_to_all(
        summed.reshape(chips, 1, (rows - 1) * LANES), "kv", 0, 0, axis_index_groups=same_core
    ).reshape(chips * (rows - 1), LANES)
    return pl.pallas_call(
        add_up,
        out_shape=jax.ShapeDtypeStruct((rows, out_proj.shape[1] // kv), jnp.bfloat16),
        in_specs=vmem_specs(1),
        compiler_params=params,
    )(parts)


def solution(mesh):
    kv = mesh.shape["kv"]
    placed = (
        P("rep", None, None),
        P("rep", "kv", None),
        P("rep"),
        P("kv", None, None),
        P("kv", None),
    )

    def device_step(*args):
        return on_device(kv, *args)

    return jax.shard_map(
        device_step, mesh=mesh, in_specs=placed, out_specs=P("rep", "kv"), check_vma=False
    )
```

```python
import jax
import jax.numpy as jnp
from jax import lax
from jax.experimental import pallas as pl
from jax.experimental.pallas import tpu as pltpu
from jax.sharding import PartitionSpec as P

LATENT = 512
LANES = 128
TILES = LATENT // LANES
HALF = LANES // 2

softmax_scale = 192.0 ** (-0.5)
masked_value = -1e30


def vmem_specs(n):
    return [pl.BlockSpec(memory_space=pltpu.VMEM)] * n


def in_hbm(x):
    return pltpu.with_memory_space_constraint(x, pltpu.HBM)


def lane_of(rows):
    return lax.broadcasted_iota(jnp.int32, (rows, LANES), 1)


def soften(s_buf, r, odd_wanted, stats):
    pairs = s_buf.shape[2] // 2
    even, odd = [
        jnp.concatenate(
            [s_buf[r, t, pl.ds(parity, pairs, stride=2), :] for t in range(s_buf.shape[1])], axis=1
        )
        for parity in range(2)
    ]
    part = jnp.where(odd_wanted, odd, even)
    top = jnp.max(part, axis=1, keepdims=True)
    exponent = jnp.where(part > 0.5 * masked_value, jnp.exp(part - top), 0.0)
    lane = lane_of(pairs)
    stats = jnp.where(lane == r, top, stats)
    stats = jnp.where(lane == HALF + r, jnp.sum(exponent, axis=1, keepdims=True), stats)
    return exponent.astype(jnp.bfloat16), stats


def weigh(out, weights, k_buf, r):
    rows = k_buf.shape[0]
    pairs = weights.shape[0]
    numerators = lax.dot_general(
        weights, k_buf[r, :LATENT, :], (((1,), (1,)), ((), ())), preferred_element_type=jnp.float32
    )
    for t in range(TILES):
        out[pl.ds(t * rows + r, pairs, stride=rows * TILES + 1), :] = numerators[
            :, t * LANES : (t + 1) * LANES
        ]


def finish(out, s_buf, k_buf, odd_wanted):
    rows = k_buf.shape[0]
    pairs = s_buf.shape[2] // 2
    stats = jnp.zeros((pairs, LANES), jnp.float32)
    weights = []
    for r in range(rows):
        exponent, stats = soften(s_buf, r, odd_wanted, stats)
        weights.append(exponent)
    for r in range(rows):
        weigh(out, weights[r], k_buf, r)
    out[pl.ds(rows * TILES, pairs, stride=rows * TILES + 1), :] = stats


def attend_theirs(lengths, queries, cache, theirs, s_buf, k_buf, l_buf, q_buf, arrived):
    rows, heads, _ = queries.shape
    shard_len = cache.shape[2]
    me = lax.axis_index("kv")
    first_core = lax.rem(me, 2) == 0
    small = [
        pltpu.make_async_copy(lengths, l_buf, arrived.at[rows]),
        pltpu.make_async_copy(queries, q_buf, arrived.at[rows + 1]),
    ]
    large = [pltpu.make_async_copy(cache.at[r], k_buf.at[r], arrived.at[r]) for r in range(rows)]
    for copy in small + large:
        copy.start()
    position = me * shard_len + lax.broadcasted_iota(jnp.int32, (1, shard_len), 1)
    stats = [jnp.zeros((heads // 2, LANES), jnp.float32)]
    weights = {}

    def score(r):
        scores = jnp.dot(q_buf[r], k_buf[r], preferred_element_type=jnp.float32) * softmax_scale
        scores = jnp.where(position < l_buf[r], scores, masked_value)
        for t in range(shard_len // LANES):
            s_buf[r, t] = scores[:, t * LANES : (t + 1) * LANES]

    def exponents(r):
        weights[r], stats[0] = soften(s_buf, r, first_core, stats[0])

    def numerators(r):
        weigh(theirs, weights[r], k_buf, r)

    for copy in small:
        copy.wait()
    parts = [range(4), range(4, rows)]
    for step in range(4):
        if step < 2:
            for r in parts[step]:
                large[r].wait()
        for part, stage in ((step - 2, numerators), (step - 1, exponents), (step, score)):
            if 0 <= part < 2:
                for r in parts[part]:
                    stage(r)
    theirs[pl.ds(rows * TILES, heads // 2, stride=rows * TILES + 1), :] = stats[0]


def attend_mine(s_buf, k_buf, mine):
    finish(mine, s_buf, k_buf, lax.rem(lax.axis_index("kv"), 2) == 1)


def merge_cores(rows, order, got, mine, merged):
    sent = rows * TILES + 1
    chips = len(order)
    stats = [ref[pl.ds(rows * TILES, chips, stride=sent), :] for ref in (got, mine)]
    top = jnp.maximum(*stats)
    weights = [jnp.exp(s - top) for s in stats]
    total = sum(pltpu.roll(s, HALF, 1) * w for s, w in zip(stats, weights))
    both = jnp.where(lane_of(chips) < HALF, top, pltpu.roll(total, HALF, 1))
    columns = [jnp.transpose(w)[:rows] for w in weights]
    for slot, q in enumerate(order):
        factors = [jnp.broadcast_to(c[:, q : q + 1], (rows, LANES)) for c in columns]
        for t in range(TILES):
            at = pl.ds(q * sent + t * rows, rows)
            merged[slot * sent + t * rows : slot * sent + (t + 1) * rows, :] = (
                got[at, :] * factors[0] + mine[at, :] * factors[1]
            )
        merged[slot * sent + TILES * rows : (slot + 1) * sent, :] = both[q : q + 1]


def project(rows, order, got, value_up, out_proj, theirs, mine):
    sent = rows * TILES + 1
    chips = got.shape[0] // sent
    features = out_proj.shape[1] // (2 * chips)
    core = lax.rem(lax.axis_index("kv"), 2)
    stats = got[pl.ds(TILES * rows, chips, stride=sent), :]
    weight = jnp.exp(stats - jnp.max(stats, axis=0, keepdims=True))
    total = jnp.sum(weight * pltpu.roll(stats, HALF, 1), axis=0, keepdims=True)
    total = jnp.transpose(jnp.broadcast_to(total, (rows, LANES)))[:rows, :1]
    combined = [
        jnp.concatenate(
            [
                jnp.sum(
                    got[pl.ds(t * rows + r, chips, stride=sent), :] * weight[:, r : r + 1],
                    axis=0,
                    keepdims=True,
                )
                for r in range(rows)
            ],
            axis=0,
        )
        for t in range(TILES)
    ]
    head_values = jnp.dot(
        jnp.concatenate(combined, axis=1).astype(jnp.bfloat16),
        value_up[0],
        preferred_element_type=jnp.float32,
    )
    projection = jnp.dot(
        (head_values / total).astype(jnp.bfloat16), out_proj[...], preferred_element_type=jnp.float32
    )
    spare = LANES - features
    lane = lane_of(rows)
    pad = jnp.zeros((rows, spare), jnp.float32)
    for slot, q in enumerate(order):
        blocks = []
        for d in (2 * q, 2 * q + 1):
            part = jnp.concatenate([projection[:, d * features : (d + 1) * features], pad], axis=1)
            last = jnp.broadcast_to(part[rows - 1 :], (rows, LANES))
            last = pltpu.roll(last, spare, 1, stride=spare, stride_axis=0)
            blocks.append(jnp.where(lane < features, part, last))
        at = pl.ds(slot * (rows - 1), rows - 1)
        theirs[at, :] = jnp.where(core == 0, blocks[1], blocks[0])[: rows - 1]
        mine[at, :] = jnp.where(core == 0, blocks[0], blocks[1])[: rows - 1]


def add_other(both, mine, out):
    out[...] = mine[...] + both[1 - lax.rem(lax.axis_index("kv"), 2)]


def add_up(got, out):
    rows, features = out.shape
    spare = LANES - features
    total = got[pl.ds(0, rows - 1), :]
    for j in range(1, got.shape[0] // (rows - 1)):
        total += got[pl.ds(j * (rows - 1), rows - 1), :]
    last = [total[i : i + 1, features:] for i in reversed(range(rows - 1))]
    out[...] = jnp.concatenate(
        [total[:, :features], jnp.concatenate(last, axis=1)], axis=0
    ).astype(out.dtype)


def core_swap(x, kv):
    return lax.ppermute(x, "kv", [(i, i ^ 1) for i in range(kv)])


def chips_from(first, chips):
    return [(first + i) % chips for i in range(chips)]


def on_device(kv, queries, latent_cache, lengths, value_up, out_proj):
    rows, heads, width = queries.shape
    shard_len = latent_cache.shape[1]
    chips = kv // 2
    orders = [chips_from(first, chips) for first in (26, 19)]
    same_core = [[[2 * i + c for i in order] for c in range(2)] for order in orders]
    params = pltpu.CompilerParams(vmem_limit_bytes=8 * 2**20)
    f32 = jnp.float32

    sent = rows * TILES + 1
    partials = jax.ShapeDtypeStruct((chips * sent, LANES), f32)
    theirs, scores, held = pl.pallas_call(
        attend_theirs,
        out_shape=[
            partials,
            jax.ShapeDtypeStruct((rows, shard_len // LANES, heads, LANES), f32),
            jax.ShapeDtypeStruct((rows, width, shard_len), latent_cache.dtype),
        ],
        in_specs=[pl.BlockSpec(memory_space=pltpu.HBM)] * 3,
        out_specs=vmem_specs(3),
        scratch_shapes=[
            pltpu.SMEM((rows,), lengths.dtype),
            pltpu.VMEM((rows, heads, width), queries.dtype),
            pltpu.SemaphoreType.DMA((rows + 2,)),
        ],
        compiler_params=params,
    )(*[in_hbm(v) for v in (lengths, queries, latent_cache.transpose(0, 2, 1))])
    got = core_swap(theirs, kv)
    mine = pl.pallas_call(
        attend_mine,
        out_shape=partials,
        in_specs=vmem_specs(2),
        out_specs=vmem_specs(1)[0],
        compiler_params=params,
    )(scores, held)
    merged = pl.pallas_call(
        lambda *refs: merge_cores(rows, orders[0], *refs),
        out_shape=partials,
        in_specs=vmem_specs(2),
        out_specs=vmem_specs(1)[0],
        compiler_params=params,
    )(got, mine)
    got = lax.all_to_all(
        merged.reshape(chips, 1, sent * LANES), "kv", 0, 0, axis_index_groups=same_core[0]
    ).reshape(chips * sent, LANES)
    features = jax.ShapeDtypeStruct((chips * (rows - 1), LANES), f32)
    theirs, mine = pl.pallas_call(
        lambda *refs: project(rows, orders[1], *refs),
        out_shape=[features] * 2,
        in_specs=vmem_specs(3),
        out_specs=vmem_specs(2),
        compiler_params=params,
    )(got, value_up, out_proj)
    both = lax.all_gather(
        theirs, "kv", axis_index_groups=[[2 * i, 2 * i + 1] for i in range(chips)]
    )
    summed = pl.pallas_call(
        add_other,
        out_shape=features,
        in_specs=vmem_specs(2),
        out_specs=vmem_specs(1)[0],
        compiler_params=params,
    )(both, mine)
    parts = lax.all_to_all(
        summed.reshape(chips, 1, (rows - 1) * LANES), "kv", 0, 0, axis_index_groups=same_core[1]
    ).reshape(chips * (rows - 1), LANES)
    return pl.pallas_call(
        add_up,
        out_shape=jax.ShapeDtypeStruct((rows, out_proj.shape[1] // kv), jnp.bfloat16),
        in_specs=vmem_specs(1),
        compiler_params=params,
    )(parts)


def solution(mesh):
    kv = mesh.shape["kv"]
    placed = (
        P("rep", None, None),
        P("rep", "kv", None),
        P("rep"),
        P("kv", None, None),
        P("kv", None),
    )

    def device_step(*args):
        return on_device(kv, *args)

    return jax.shard_map(
        device_step, mesh=mesh, in_specs=placed, out_specs=P("rep", "kv"), check_vma=False
    )
```

```python
import jax
import jax.numpy as jnp
from jax import lax
from jax.experimental import pallas as pl
from jax.experimental.pallas import tpu as pltpu
from jax.sharding import PartitionSpec as P

LATENT = 512
LANES = 128
TILES = LATENT // LANES
HALF = LANES // 2

softmax_scale = 192.0 ** (-0.5)
masked_value = -1e30


def vmem_specs(n):
    return [pl.BlockSpec(memory_space=pltpu.VMEM)] * n


def in_hbm(x):
    return pltpu.with_memory_space_constraint(x, pltpu.HBM)


def lane_of(rows):
    return lax.broadcasted_iota(jnp.int32, (rows, LANES), 1)


def soften(s_buf, r, odd_wanted, stats):
    pairs = s_buf.shape[2] // 2
    even, odd = [
        jnp.concatenate(
            [s_buf[r, t, pl.ds(parity, pairs, stride=2), :] for t in range(s_buf.shape[1])], axis=1
        )
        for parity in range(2)
    ]
    part = jnp.where(odd_wanted, odd, even)
    top = jnp.max(part, axis=1, keepdims=True)
    exponent = jnp.where(part > 0.5 * masked_value, jnp.exp(part - top), 0.0)
    lane = lane_of(pairs)
    stats = jnp.where(lane == r, top, stats)
    stats = jnp.where(lane == HALF + r, jnp.sum(exponent, axis=1, keepdims=True), stats)
    return exponent.astype(jnp.bfloat16), stats


def weigh(out, weights, k_buf, r):
    rows = k_buf.shape[0]
    pairs = weights.shape[0]
    numerators = lax.dot_general(
        weights, k_buf[r, :LATENT, :], (((1,), (1,)), ((), ())), preferred_element_type=jnp.float32
    )
    for t in range(TILES):
        out[pl.ds(t * rows + r, pairs, stride=rows * TILES + 1), :] = numerators[
            :, t * LANES : (t + 1) * LANES
        ]


def finish(out, s_buf, k_buf, odd_wanted):
    rows = k_buf.shape[0]
    pairs = s_buf.shape[2] // 2
    stats = jnp.zeros((pairs, LANES), jnp.float32)
    weights = []
    for r in range(rows):
        exponent, stats = soften(s_buf, r, odd_wanted, stats)
        weights.append(exponent)
    for r in range(rows):
        weigh(out, weights[r], k_buf, r)
    out[pl.ds(rows * TILES, pairs, stride=rows * TILES + 1), :] = stats


def attend_theirs(lengths, queries, cache, theirs, s_buf, k_buf, l_buf, q_buf, arrived):
    rows, heads, _ = queries.shape
    shard_len = cache.shape[2]
    me = lax.axis_index("kv")
    first_core = lax.rem(me, 2) == 0
    small = [
        pltpu.make_async_copy(lengths, l_buf, arrived.at[rows]),
        pltpu.make_async_copy(queries, q_buf, arrived.at[rows + 1]),
    ]
    large = [pltpu.make_async_copy(cache.at[r], k_buf.at[r], arrived.at[r]) for r in range(rows)]
    for copy in small + large:
        copy.start()
    position = me * shard_len + lax.broadcasted_iota(jnp.int32, (1, shard_len), 1)
    stats = [jnp.zeros((heads // 2, LANES), jnp.float32)]
    weights = {}

    def score(r):
        scores = jnp.dot(q_buf[r], k_buf[r], preferred_element_type=jnp.float32) * softmax_scale
        scores = jnp.where(position < l_buf[r], scores, masked_value)
        for t in range(shard_len // LANES):
            s_buf[r, t] = scores[:, t * LANES : (t + 1) * LANES]

    def exponents(r):
        weights[r], stats[0] = soften(s_buf, r, first_core, stats[0])

    def numerators(r):
        weigh(theirs, weights[r], k_buf, r)

    for copy in small:
        copy.wait()
    parts = [range(4), range(4, rows)]
    for step in range(4):
        if step < 2:
            for r in parts[step]:
                large[r].wait()
        for part, stage in ((step - 2, numerators), (step - 1, exponents), (step, score)):
            if 0 <= part < 2:
                for r in parts[part]:
                    stage(r)
    theirs[pl.ds(rows * TILES, heads // 2, stride=rows * TILES + 1), :] = stats[0]


def attend_mine(s_buf, k_buf, mine):
    finish(mine, s_buf, k_buf, lax.rem(lax.axis_index("kv"), 2) == 1)


def merge_cores(rows, order, got, mine, merged):
    sent = rows * TILES + 1
    chips = len(order)
    stats = [ref[pl.ds(rows * TILES, chips, stride=sent), :] for ref in (got, mine)]
    top = jnp.maximum(*stats)
    weights = [jnp.exp(s - top) for s in stats]
    total = sum(pltpu.roll(s, HALF, 1) * w for s, w in zip(stats, weights))
    both = jnp.where(lane_of(chips) < HALF, top, pltpu.roll(total, HALF, 1))
    spans, slot = [], 0
    while slot < chips:
        q = order[slot]
        span = chips - q if slot == 0 else chips - slot
        spans.append((q, slot, span))
        slot += span
    for r in range(rows):
        columns = [jnp.broadcast_to(w[:, r : r + 1], (chips, LANES)) for w in weights]
        for t in range(TILES):
            row = t * rows + r
            for q, slot, span in spans:
                at = pl.ds(q * sent + row, span, stride=sent)
                merged[pl.ds(slot * sent + row, span, stride=sent), :] = (
                    got[at, :] * columns[0][q : q + span] + mine[at, :] * columns[1][q : q + span]
                )
    for q, slot, span in spans:
        merged[pl.ds((slot + 1) * sent - 1, span, stride=sent), :] = both[q : q + span]


def project(rows, order, got, value_up, out_proj, theirs, mine):
    sent = rows * TILES + 1
    chips = got.shape[0] // sent
    features = out_proj.shape[1] // (2 * chips)
    core = lax.rem(lax.axis_index("kv"), 2)
    stats = got[pl.ds(TILES * rows, chips, stride=sent), :]
    weight = jnp.exp(stats - jnp.max(stats, axis=0, keepdims=True))
    total = jnp.sum(weight * pltpu.roll(stats, HALF, 1), axis=0, keepdims=True)
    total = jnp.transpose(jnp.broadcast_to(total, (rows, LANES)))[:rows, :1]
    combined = [
        jnp.concatenate(
            [
                jnp.sum(
                    got[pl.ds(t * rows + r, chips, stride=sent), :] * weight[:, r : r + 1],
                    axis=0,
                    keepdims=True,
                )
                for r in range(rows)
            ],
            axis=0,
        )
        for t in range(TILES)
    ]
    head_values = jnp.dot(
        jnp.concatenate(combined, axis=1).astype(jnp.bfloat16),
        value_up[0],
        preferred_element_type=jnp.float32,
    )
    projection = jnp.dot(
        (head_values / total).astype(jnp.bfloat16), out_proj[...], preferred_element_type=jnp.float32
    )
    spare = LANES - features
    lane = lane_of(rows)
    pad = jnp.zeros((rows, spare), jnp.float32)
    for slot, q in enumerate(order):
        blocks = []
        for d in (2 * q, 2 * q + 1):
            part = jnp.concatenate([projection[:, d * features : (d + 1) * features], pad], axis=1)
            last = jnp.broadcast_to(part[rows - 1 :], (rows, LANES))
            last = pltpu.roll(last, spare, 1, stride=spare, stride_axis=0)
            blocks.append(jnp.where(lane < features, part, last))
        at = pl.ds(slot * (rows - 1), rows - 1)
        theirs[at, :] = jnp.where(core == 0, blocks[1], blocks[0])[: rows - 1]
        mine[at, :] = jnp.where(core == 0, blocks[0], blocks[1])[: rows - 1]


def add_other(both, mine, out):
    out[...] = mine[...] + both[1 - lax.rem(lax.axis_index("kv"), 2)]


def add_up(got, out):
    rows, features = out.shape
    spare = LANES - features
    parts = [got[pl.ds(j, rows - 1), :] for j in range(0, got.shape[0], rows - 1)]
    while len(parts) > 1:
        parts = [sum(parts[i : i + 2]) for i in range(0, len(parts), 2)]
    total = parts[0]
    last = [total[i : i + 1, features:] for i in reversed(range(rows - 1))]
    out[...] = jnp.concatenate(
        [total[:, :features], jnp.concatenate(last, axis=1)], axis=0
    ).astype(out.dtype)


def core_swap(x, kv):
    return lax.ppermute(x, "kv", [(i, i ^ 1) for i in range(kv)])


def chips_from(first, chips):
    return [(first + i) % chips for i in range(chips)]


def on_device(kv, queries, latent_cache, lengths, value_up, out_proj):
    rows, heads, width = queries.shape
    shard_len = latent_cache.shape[1]
    chips = kv // 2
    orders = [chips_from(first, chips) for first in (26, 19)]
    same_core = [[[2 * i + c for i in order] for c in range(2)] for order in orders]
    params = pltpu.CompilerParams(vmem_limit_bytes=8 * 2**20)
    f32 = jnp.float32

    sent = rows * TILES + 1
    partials = jax.ShapeDtypeStruct((chips * sent, LANES), f32)
    theirs, scores, held = pl.pallas_call(
        attend_theirs,
        out_shape=[
            partials,
            jax.ShapeDtypeStruct((rows, shard_len // LANES, heads, LANES), f32),
            jax.ShapeDtypeStruct((rows, width, shard_len), latent_cache.dtype),
        ],
        in_specs=[pl.BlockSpec(memory_space=pltpu.HBM)] * 3,
        out_specs=vmem_specs(3),
        scratch_shapes=[
            pltpu.SMEM((rows,), lengths.dtype),
            pltpu.VMEM((rows, heads, width), queries.dtype),
            pltpu.SemaphoreType.DMA((rows + 2,)),
        ],
        compiler_params=params,
    )(*[in_hbm(v) for v in (lengths, queries, latent_cache.transpose(0, 2, 1))])
    got = core_swap(theirs, kv)
    mine = pl.pallas_call(
        attend_mine,
        out_shape=partials,
        in_specs=vmem_specs(2),
        out_specs=vmem_specs(1)[0],
        compiler_params=params,
    )(scores, held)
    merged = pl.pallas_call(
        lambda *refs: merge_cores(rows, orders[0], *refs),
        out_shape=partials,
        in_specs=vmem_specs(2),
        out_specs=vmem_specs(1)[0],
        compiler_params=params,
    )(got, mine)
    got = lax.all_to_all(
        merged.reshape(chips, 1, sent * LANES), "kv", 0, 0, axis_index_groups=same_core[0]
    ).reshape(chips * sent, LANES)
    features = jax.ShapeDtypeStruct((chips * (rows - 1), LANES), f32)
    theirs, mine = pl.pallas_call(
        lambda *refs: project(rows, orders[1], *refs),
        out_shape=[features] * 2,
        in_specs=vmem_specs(3),
        out_specs=vmem_specs(2),
        compiler_params=params,
    )(got, value_up, out_proj)
    both = lax.all_gather(
        theirs, "kv", axis_index_groups=[[2 * i, 2 * i + 1] for i in range(chips)]
    )
    summed = pl.pallas_call(
        add_other,
        out_shape=features,
        in_specs=vmem_specs(2),
        out_specs=vmem_specs(1)[0],
        compiler_params=params,
    )(both, mine)
    parts = lax.all_to_all(
        summed.reshape(chips, 1, (rows - 1) * LANES), "kv", 0, 0, axis_index_groups=same_core[1]
    ).reshape(chips * (rows - 1), LANES)
    return pl.pallas_call(
        add_up,
        out_shape=jax.ShapeDtypeStruct((rows, out_proj.shape[1] // kv), jnp.bfloat16),
        in_specs=vmem_specs(1),
        compiler_params=params,
    )(parts)


def solution(mesh):
    kv = mesh.shape["kv"]
    placed = (
        P("rep", None, None),
        P("rep", "kv", None),
        P("rep"),
        P("kv", None, None),
        P("kv", None),
    )

    def device_step(*args):
        return on_device(kv, *args)

    return jax.shard_map(
        device_step, mesh=mesh, in_specs=placed, out_specs=P("rep", "kv"), check_vma=False
    )
```

```python
import jax
import jax.numpy as jnp
from jax import lax
from jax.experimental import pallas as pl
from jax.experimental.pallas import tpu as pltpu
from jax.sharding import PartitionSpec as P

LATENT = 512
LANES = 128
TILES = LATENT // LANES
HALF = LANES // 2

softmax_scale = 192.0 ** (-0.5)
masked_value = -1e30


def vmem_specs(n):
    return [pl.BlockSpec(memory_space=pltpu.VMEM)] * n


def in_hbm(x):
    return pltpu.with_memory_space_constraint(x, pltpu.HBM)


def lane_of(rows):
    return lax.broadcasted_iota(jnp.int32, (rows, LANES), 1)


def soften(s_buf, r, odd_wanted, stats):
    pairs = s_buf.shape[2] // 2
    even, odd = [
        jnp.concatenate(
            [s_buf[r, t, pl.ds(parity, pairs, stride=2), :] for t in range(s_buf.shape[1])], axis=1
        )
        for parity in range(2)
    ]
    part = jnp.where(odd_wanted, odd, even)
    top = jnp.max(part, axis=1, keepdims=True)
    exponent = jnp.where(part > 0.5 * masked_value, jnp.exp(part - top), 0.0)
    lane = lane_of(pairs)
    stats = jnp.where(lane == r, top, stats)
    stats = jnp.where(lane == HALF + r, jnp.sum(exponent, axis=1, keepdims=True), stats)
    return exponent.astype(jnp.bfloat16), stats


def weigh(out, weights, k_buf, r):
    rows = k_buf.shape[0]
    pairs = weights.shape[0]
    numerators = lax.dot_general(
        weights, k_buf[r, :LATENT, :], (((1,), (1,)), ((), ())), preferred_element_type=jnp.float32
    )
    for t in range(TILES):
        out[pl.ds(t * rows + r, pairs, stride=rows * TILES + 1), :] = numerators[
            :, t * LANES : (t + 1) * LANES
        ]


def finish(out, s_buf, k_buf, odd_wanted):
    rows = k_buf.shape[0]
    pairs = s_buf.shape[2] // 2
    stats = jnp.zeros((pairs, LANES), jnp.float32)
    weights = []
    for r in range(rows):
        exponent, stats = soften(s_buf, r, odd_wanted, stats)
        weights.append(exponent)
    for r in range(rows):
        weigh(out, weights[r], k_buf, r)
    out[pl.ds(rows * TILES, pairs, stride=rows * TILES + 1), :] = stats


def attend_theirs(lengths, queries, cache, theirs, s_buf, k_buf, l_buf, q_buf, arrived):
    rows, heads, _ = queries.shape
    shard_len = cache.shape[2]
    me = lax.axis_index("kv")
    first_core = lax.rem(me, 2) == 0
    small = [
        pltpu.make_async_copy(lengths, l_buf, arrived.at[rows]),
        pltpu.make_async_copy(queries, q_buf, arrived.at[rows + 1]),
    ]
    large = [pltpu.make_async_copy(cache.at[r], k_buf.at[r], arrived.at[r]) for r in range(rows)]
    for copy in small + large:
        copy.start()
    position = me * shard_len + lax.broadcasted_iota(jnp.int32, (1, shard_len), 1)
    stats = [jnp.zeros((heads // 2, LANES), jnp.float32)]
    weights = {}

    def score(r):
        scores = jnp.dot(q_buf[r], k_buf[r], preferred_element_type=jnp.float32) * softmax_scale
        scores = jnp.where(position < l_buf[r], scores, masked_value)
        for t in range(shard_len // LANES):
            s_buf[r, t] = scores[:, t * LANES : (t + 1) * LANES]

    def exponents(r):
        weights[r], stats[0] = soften(s_buf, r, first_core, stats[0])

    def numerators(r):
        weigh(theirs, weights[r], k_buf, r)

    for copy in small:
        copy.wait()
    parts = [range(4), range(4, rows)]
    for step in range(4):
        if step < 2:
            for r in parts[step]:
                large[r].wait()
        for part, stage in ((step - 2, numerators), (step - 1, exponents), (step, score)):
            if 0 <= part < 2:
                for r in parts[part]:
                    stage(r)
    theirs[pl.ds(rows * TILES, heads // 2, stride=rows * TILES + 1), :] = stats[0]


def attend_mine(s_buf, k_buf, mine):
    finish(mine, s_buf, k_buf, lax.rem(lax.axis_index("kv"), 2) == 1)


def merge_cores(rows, order, got, mine, merged):
    sent = rows * TILES + 1
    chips = len(order)
    stats = [ref[pl.ds(rows * TILES, chips, stride=sent), :] for ref in (got, mine)]
    top = jnp.maximum(*stats)
    weights = [jnp.exp(s - top) for s in stats]
    total = sum(pltpu.roll(s, HALF, 1) * w for s, w in zip(stats, weights))
    both = jnp.where(lane_of(chips) < HALF, top, pltpu.roll(total, HALF, 1))
    columns = [jnp.transpose(w)[:rows] for w in weights]
    turned = jnp.concatenate([both[order[0] :], both[: order[0]]], axis=0)
    merged[pl.ds(rows * TILES, chips, stride=sent), :] = turned
    for slot, q in enumerate(order):
        factors = [jnp.broadcast_to(c[:, q : q + 1], (rows, LANES)) for c in columns]
        for t in range(TILES):
            at = pl.ds(q * sent + t * rows, rows)
            merged[slot * sent + t * rows : slot * sent + (t + 1) * rows, :] = (
                got[at, :] * factors[0] + mine[at, :] * factors[1]
            )


def project(rows, order, got, value_up, out_proj, theirs, mine):
    sent = rows * TILES + 1
    chips = got.shape[0] // sent
    features = out_proj.shape[1] // (2 * chips)
    core = lax.rem(lax.axis_index("kv"), 2)
    stats = got[pl.ds(TILES * rows, chips, stride=sent), :]
    weight = jnp.exp(stats - jnp.max(stats, axis=0, keepdims=True))
    total = jnp.sum(weight * pltpu.roll(stats, HALF, 1), axis=0, keepdims=True)
    total = jnp.transpose(jnp.broadcast_to(total, (rows, LANES)))[:rows, :1]
    combined = [
        jnp.concatenate(
            [
                jnp.sum(
                    got[pl.ds(t * rows + r, chips, stride=sent), :] * weight[:, r : r + 1],
                    axis=0,
                    keepdims=True,
                )
                for r in range(rows)
            ],
            axis=0,
        )
        for t in range(TILES)
    ]
    head_values = jnp.dot(
        jnp.concatenate(combined, axis=1).astype(jnp.bfloat16),
        value_up[0],
        preferred_element_type=jnp.float32,
    )
    projection = jnp.dot(
        (head_values / total).astype(jnp.bfloat16), out_proj[...], preferred_element_type=jnp.float32
    )
    spare = LANES - features
    lane = lane_of(rows)
    pad = jnp.zeros((rows, spare), jnp.float32)
    for slot, q in enumerate(order):
        blocks = []
        for d in (2 * q, 2 * q + 1):
            part = jnp.concatenate([projection[:, d * features : (d + 1) * features], pad], axis=1)
            last = jnp.broadcast_to(part[rows - 1 :], (rows, LANES))
            last = pltpu.roll(last, spare, 1, stride=spare, stride_axis=0)
            blocks.append(jnp.where(lane < features, part, last))
        at = pl.ds(slot * (rows - 1), rows - 1)
        theirs[at, :] = jnp.where(core == 0, blocks[1], blocks[0])[: rows - 1]
        mine[at, :] = jnp.where(core == 0, blocks[0], blocks[1])[: rows - 1]


def add_other(both, mine, out):
    at = pl.ds(0, out.shape[0])
    out[...] = mine[at, :] + both[1 - lax.rem(lax.axis_index("kv"), 2), at, :]


def add_up(got, out):
    rows, features = out.shape
    spare = LANES - features
    count = got.shape[0]
    parts = [got[pl.ds(j, rows - 1), :] for j in range(0, count - rows + 1, rows - 1)]
    parts.append(got[pl.ds(count - rows, rows), :][1:])
    while len(parts) > 1:
        parts = [sum(parts[i : i + 2]) for i in range(0, len(parts), 2)]
    total = parts[0]
    last = [total[i : i + 1, features:] for i in reversed(range(rows - 1))]
    out[...] = jnp.concatenate(
        [total[:, :features], jnp.concatenate(last, axis=1)], axis=0
    ).astype(out.dtype)


def core_swap(x, kv):
    return lax.ppermute(x, "kv", [(i, i ^ 1) for i in range(kv)])


def chips_from(first, chips):
    return [(first + i) % chips for i in range(chips)]


def on_device(kv, queries, latent_cache, lengths, value_up, out_proj):
    rows, heads, width = queries.shape
    shard_len = latent_cache.shape[1]
    chips = kv // 2
    orders = [chips_from(first, chips) for first in (26, 19)]
    same_core = [[[2 * i + c for i in order] for c in range(2)] for order in orders]
    params = pltpu.CompilerParams(vmem_limit_bytes=8 * 2**20)
    f32 = jnp.float32

    sent = rows * TILES + 1
    partials = jax.ShapeDtypeStruct((chips * sent, LANES), f32)
    theirs, scores, held = pl.pallas_call(
        attend_theirs,
        out_shape=[
            partials,
            jax.ShapeDtypeStruct((rows, shard_len // LANES, heads, LANES), f32),
            jax.ShapeDtypeStruct((rows, width, shard_len), latent_cache.dtype),
        ],
        in_specs=[pl.BlockSpec(memory_space=pltpu.HBM)] * 3,
        out_specs=vmem_specs(3),
        scratch_shapes=[
            pltpu.SMEM((rows,), lengths.dtype),
            pltpu.VMEM((rows, heads, width), queries.dtype),
            pltpu.SemaphoreType.DMA((rows + 2,)),
        ],
        compiler_params=params,
    )(*[in_hbm(v) for v in (lengths, queries, latent_cache.transpose(0, 2, 1))])
    got = core_swap(theirs, kv)
    mine = pl.pallas_call(
        attend_mine,
        out_shape=partials,
        in_specs=vmem_specs(2),
        out_specs=vmem_specs(1)[0],
        compiler_params=params,
    )(scores, held)
    merged = pl.pallas_call(
        lambda *refs: merge_cores(rows, orders[0], *refs),
        out_shape=partials,
        in_specs=vmem_specs(2),
        out_specs=vmem_specs(1)[0],
        compiler_params=params,
    )(got, mine)
    got = lax.all_to_all(
        merged.reshape(chips, 1, sent * LANES), "kv", 0, 0, axis_index_groups=same_core[0]
    ).reshape(chips * sent, LANES)
    packed = jax.ShapeDtypeStruct((chips * (rows - 1), LANES), f32)
    features = jax.ShapeDtypeStruct((chips * (rows - 1) + rows, LANES), f32)
    theirs, mine = pl.pallas_call(
        lambda *refs: project(rows, orders[1], *refs),
        out_shape=[features] * 2,
        in_specs=vmem_specs(3),
        out_specs=vmem_specs(2),
        compiler_params=params,
    )(got, value_up, out_proj)
    both = lax.all_gather(
        theirs, "kv", axis_index_groups=[[2 * i, 2 * i + 1] for i in range(chips)]
    )
    summed = pl.pallas_call(
        add_other,
        out_shape=packed,
        in_specs=vmem_specs(2),
        out_specs=vmem_specs(1)[0],
        compiler_params=params,
    )(both, mine)
    parts = lax.all_to_all(
        summed.reshape(chips, 1, (rows - 1) * LANES), "kv", 0, 0, axis_index_groups=same_core[1]
    ).reshape(chips * (rows - 1), LANES)
    return pl.pallas_call(
        add_up,
        out_shape=jax.ShapeDtypeStruct((rows, out_proj.shape[1] // kv), jnp.bfloat16),
        in_specs=vmem_specs(1),
        compiler_params=params,
    )(parts)


def solution(mesh):
    kv = mesh.shape["kv"]
    placed = (
        P("rep", None, None),
        P("rep", "kv", None),
        P("rep"),
        P("kv", None, None),
        P("kv", None),
    )

    def device_step(*args):
        return on_device(kv, *args)

    return jax.shard_map(
        device_step, mesh=mesh, in_specs=placed, out_specs=P("rep", "kv"), check_vma=False
    )
```

```python
import jax
import jax.numpy as jnp
from jax import lax
from jax.experimental import pallas as pl
from jax.experimental.pallas import tpu as pltpu
from jax.sharding import PartitionSpec as P

LATENT = 512
LANES = 128
TILES = LATENT // LANES
HALF = LANES // 2

softmax_scale = 192.0 ** (-0.5)
masked_value = -1e30


def vmem_specs(n):
    return [pl.BlockSpec(memory_space=pltpu.VMEM)] * n


def in_hbm(x):
    return pltpu.with_memory_space_constraint(x, pltpu.HBM)


def lane_of(rows):
    return lax.broadcasted_iota(jnp.int32, (rows, LANES), 1)


def soften(s_buf, r, odd_wanted, stats, first):
    pairs = s_buf.shape[2] // 2
    even, odd = [
        jnp.concatenate(
            [s_buf[r, t, pl.ds(parity, pairs, stride=2), :] for t in range(s_buf.shape[1])], axis=1
        )
        for parity in range(2)
    ]
    part = jnp.where(odd_wanted, odd, even)
    part = jnp.concatenate([part[first:], part[:first]], axis=0)
    top = jnp.max(part, axis=1, keepdims=True)
    exponent = jnp.where(part > 0.5 * masked_value, jnp.exp(part - top), 0.0)
    lane = lane_of(pairs)
    stats = jnp.where(lane == r, top, stats)
    stats = jnp.where(lane == HALF + r, jnp.sum(exponent, axis=1, keepdims=True), stats)
    return exponent.astype(jnp.bfloat16), stats


def weigh(out, weights, k_buf, r):
    rows = k_buf.shape[0]
    pairs = weights.shape[0]
    numerators = lax.dot_general(
        weights, k_buf[r, :LATENT, :], (((1,), (1,)), ((), ())), preferred_element_type=jnp.float32
    )
    for t in range(TILES):
        out[pl.ds(t * rows + r, pairs, stride=rows * TILES + 1), :] = numerators[
            :, t * LANES : (t + 1) * LANES
        ]


def finish(out, s_buf, k_buf, odd_wanted, first):
    rows = k_buf.shape[0]
    pairs = s_buf.shape[2] // 2
    stats = jnp.zeros((pairs, LANES), jnp.float32)
    weights = []
    for r in range(rows):
        exponent, stats = soften(s_buf, r, odd_wanted, stats, first)
        weights.append(exponent)
    for r in range(rows):
        weigh(out, weights[r], k_buf, r)
    out[pl.ds(rows * TILES, pairs, stride=rows * TILES + 1), :] = stats


def attend_theirs(first, lengths, queries, cache, theirs, s_buf, k_buf, l_buf, q_buf, arrived):
    rows, heads, _ = queries.shape
    shard_len = cache.shape[2]
    me = lax.axis_index("kv")
    first_core = lax.rem(me, 2) == 0
    small = [
        pltpu.make_async_copy(lengths, l_buf, arrived.at[rows]),
        pltpu.make_async_copy(queries, q_buf, arrived.at[rows + 1]),
    ]
    large = [pltpu.make_async_copy(cache.at[r], k_buf.at[r], arrived.at[r]) for r in range(rows)]
    for copy in small + large:
        copy.start()
    position = me * shard_len + lax.broadcasted_iota(jnp.int32, (1, shard_len), 1)
    stats = [jnp.zeros((heads // 2, LANES), jnp.float32)]
    weights = {}

    def score(r):
        scores = jnp.dot(q_buf[r], k_buf[r], preferred_element_type=jnp.float32) * softmax_scale
        scores = jnp.where(position < l_buf[r], scores, masked_value)
        for t in range(shard_len // LANES):
            s_buf[r, t] = scores[:, t * LANES : (t + 1) * LANES]

    def exponents(r):
        weights[r], stats[0] = soften(s_buf, r, first_core, stats[0], first)

    def numerators(r):
        weigh(theirs, weights[r], k_buf, r)

    for copy in small:
        copy.wait()
    parts = [range(4), range(4, rows)]
    for step in range(4):
        if step < 2:
            for r in parts[step]:
                large[r].wait()
        for part, stage in ((step - 2, numerators), (step - 1, exponents), (step, score)):
            if 0 <= part < 2:
                for r in parts[part]:
                    stage(r)
    theirs[pl.ds(rows * TILES, heads // 2, stride=rows * TILES + 1), :] = stats[0]


def attend_mine(first, s_buf, k_buf, mine):
    finish(mine, s_buf, k_buf, lax.rem(lax.axis_index("kv"), 2) == 1, first)


def merge_cores(rows, got, mine, merged):
    sent = rows * TILES + 1
    chips = got.shape[0] // sent
    last = pl.ds(rows * TILES, chips, stride=sent)
    stats = [got[last, :], mine[last, :]]
    top = jnp.maximum(*stats)
    weights = [jnp.exp(s - top) for s in stats]
    total = sum(pltpu.roll(s, HALF, 1) * w for s, w in zip(stats, weights))
    merged[last, :] = jnp.where(lane_of(chips) < HALF, top, pltpu.roll(total, HALF, 1))
    for r in range(rows):
        columns = [jnp.broadcast_to(w[:, r : r + 1], (chips, LANES)) for w in weights]
        for t in range(TILES):
            at = pl.ds(t * rows + r, chips, stride=sent)
            merged[at, :] = got[at, :] * columns[0] + mine[at, :] * columns[1]


def project(rows, order, got, value_up, out_proj, theirs, mine):
    sent = rows * TILES + 1
    chips = got.shape[0] // sent
    features = out_proj.shape[1] // (2 * chips)
    core = lax.rem(lax.axis_index("kv"), 2)
    stats = got[pl.ds(TILES * rows, chips, stride=sent), :]
    weight = jnp.exp(stats - jnp.max(stats, axis=0, keepdims=True))
    total = jnp.sum(weight * pltpu.roll(stats, HALF, 1), axis=0, keepdims=True)
    total = jnp.transpose(jnp.broadcast_to(total, (rows, LANES)))[:rows, :1]
    combined = [
        jnp.concatenate(
            [
                jnp.sum(
                    got[pl.ds(t * rows + r, chips, stride=sent), :] * weight[:, r : r + 1],
                    axis=0,
                    keepdims=True,
                )
                for r in range(rows)
            ],
            axis=0,
        )
        for t in range(TILES)
    ]
    head_values = jnp.dot(
        jnp.concatenate(combined, axis=1).astype(jnp.bfloat16),
        value_up[0],
        preferred_element_type=jnp.float32,
    )
    projection = jnp.dot(
        (head_values / total).astype(jnp.bfloat16), out_proj[...], preferred_element_type=jnp.float32
    )
    spare = LANES - features
    lane = lane_of(rows)
    pad = jnp.zeros((rows, spare), jnp.float32)
    for slot, q in enumerate(order):
        blocks = []
        for d in (2 * q, 2 * q + 1):
            part = jnp.concatenate([projection[:, d * features : (d + 1) * features], pad], axis=1)
            last = jnp.broadcast_to(part[rows - 1 :], (rows, LANES))
            last = pltpu.roll(last, spare, 1, stride=spare, stride_axis=0)
            blocks.append(jnp.where(lane < features, part, last))
        at = pl.ds(slot * (rows - 1), rows - 1)
        theirs[at, :] = jnp.where(core == 0, blocks[1], blocks[0])[: rows - 1]
        mine[at, :] = jnp.where(core == 0, blocks[0], blocks[1])[: rows - 1]


def add_other(both, mine, out):
    at = pl.ds(0, out.shape[0])
    out[...] = mine[at, :] + both[1 - lax.rem(lax.axis_index("kv"), 2), at, :]


def add_up(got, out):
    rows, features = out.shape
    spare = LANES - features
    count = got.shape[0]
    parts = [got[pl.ds(j, rows - 1), :] for j in range(0, count - rows + 1, rows - 1)]
    parts.append(got[pl.ds(count - rows, rows), :][1:])
    while len(parts) > 1:
        parts = [sum(parts[i : i + 2]) for i in range(0, len(parts), 2)]
    total = parts[0]
    last = [total[i : i + 1, features:] for i in reversed(range(rows - 1))]
    out[...] = jnp.concatenate(
        [total[:, :features], jnp.concatenate(last, axis=1)], axis=0
    ).astype(out.dtype)


def core_swap(x, kv):
    return lax.ppermute(x, "kv", [(i, i ^ 1) for i in range(kv)])


def chips_from(first, chips):
    return [(first + i) % chips for i in range(chips)]


def on_device(kv, queries, latent_cache, lengths, value_up, out_proj):
    rows, heads, width = queries.shape
    shard_len = latent_cache.shape[1]
    chips = kv // 2
    orders = [chips_from(first, chips) for first in (26, 19)]
    same_core = [[[2 * i + c for i in order] for c in range(2)] for order in orders]
    params = pltpu.CompilerParams(vmem_limit_bytes=8 * 2**20)
    f32 = jnp.float32

    sent = rows * TILES + 1
    partials = jax.ShapeDtypeStruct((chips * sent, LANES), f32)
    theirs, scores, held = pl.pallas_call(
        lambda *refs: attend_theirs(orders[0][0], *refs),
        out_shape=[
            partials,
            jax.ShapeDtypeStruct((rows, shard_len // LANES, heads, LANES), f32),
            jax.ShapeDtypeStruct((rows, width, shard_len), latent_cache.dtype),
        ],
        in_specs=[pl.BlockSpec(memory_space=pltpu.HBM)] * 3,
        out_specs=vmem_specs(3),
        scratch_shapes=[
            pltpu.SMEM((rows,), lengths.dtype),
            pltpu.VMEM((rows, heads, width), queries.dtype),
            pltpu.SemaphoreType.DMA((rows + 2,)),
        ],
        compiler_params=params,
    )(*[in_hbm(v) for v in (lengths, queries, latent_cache.transpose(0, 2, 1))])
    got = core_swap(theirs, kv)
    mine = pl.pallas_call(
        lambda *refs: attend_mine(orders[0][0], *refs),
        out_shape=partials,
        in_specs=vmem_specs(2),
        out_specs=vmem_specs(1)[0],
        compiler_params=params,
    )(scores, held)
    merged = pl.pallas_call(
        lambda *refs: merge_cores(rows, *refs),
        out_shape=partials,
        in_specs=vmem_specs(2),
        out_specs=vmem_specs(1)[0],
        compiler_params=params,
    )(got, mine)
    got = lax.all_to_all(
        merged.reshape(chips, 1, sent * LANES), "kv", 0, 0, axis_index_groups=same_core[0]
    ).reshape(chips * sent, LANES)
    packed = jax.ShapeDtypeStruct((chips * (rows - 1), LANES), f32)
    features = jax.ShapeDtypeStruct((chips * (rows - 1) + rows, LANES), f32)
    theirs, mine = pl.pallas_call(
        lambda *refs: project(rows, orders[1], *refs),
        out_shape=[features] * 2,
        in_specs=vmem_specs(3),
        out_specs=vmem_specs(2),
        compiler_params=params,
    )(got, value_up, out_proj)
    both = lax.all_gather(
        theirs, "kv", axis_index_groups=[[2 * i, 2 * i + 1] for i in range(chips)]
    )
    summed = pl.pallas_call(
        add_other,
        out_shape=packed,
        in_specs=vmem_specs(2),
        out_specs=vmem_specs(1)[0],
        compiler_params=params,
    )(both, mine)
    parts = lax.all_to_all(
        summed.reshape(chips, 1, (rows - 1) * LANES), "kv", 0, 0, axis_index_groups=same_core[1]
    ).reshape(chips * (rows - 1), LANES)
    return pl.pallas_call(
        add_up,
        out_shape=jax.ShapeDtypeStruct((rows, out_proj.shape[1] // kv), jnp.bfloat16),
        in_specs=vmem_specs(1),
        compiler_params=params,
    )(parts)


def solution(mesh):
    kv = mesh.shape["kv"]
    placed = (
        P("rep", None, None),
        P("rep", "kv", None),
        P("rep"),
        P("kv", None, None),
        P("kv", None),
    )

    def device_step(*args):
        return on_device(kv, *args)

    return jax.shard_map(
        device_step, mesh=mesh, in_specs=placed, out_specs=P("rep", "kv"), check_vma=False
    )
```

```python
import jax
import jax.numpy as jnp
from jax import lax
from jax.experimental import pallas as pl
from jax.experimental.pallas import tpu as pltpu
from jax.sharding import PartitionSpec as P

LATENT = 512
LANES = 128
TILES = LATENT // LANES
HALF = LANES // 2

softmax_scale = 192.0 ** (-0.5)
masked_value = -1e30


def vmem_specs(n):
    return [pl.BlockSpec(memory_space=pltpu.VMEM)] * n


def in_hbm(x):
    return pltpu.with_memory_space_constraint(x, pltpu.HBM)


def lane_of(rows):
    return lax.broadcasted_iota(jnp.int32, (rows, LANES), 1)


def soften(s_buf, r, odd_wanted, stats):
    pairs = s_buf.shape[2] // 2
    even, odd = [
        jnp.concatenate(
            [s_buf[r, t, pl.ds(parity, pairs, stride=2), :] for t in range(s_buf.shape[1])], axis=1
        )
        for parity in range(2)
    ]
    part = jnp.where(odd_wanted, odd, even)
    top = jnp.max(part, axis=1, keepdims=True)
    exponent = jnp.where(part > 0.5 * masked_value, jnp.exp(part - top), 0.0)
    lane = lane_of(pairs)
    stats = jnp.where(lane == r, top, stats)
    stats = jnp.where(lane == HALF + r, jnp.sum(exponent, axis=1, keepdims=True), stats)
    return exponent.astype(jnp.bfloat16), stats


def weigh(out, weights, k_buf, r):
    rows = k_buf.shape[0]
    pairs = weights.shape[0]
    numerators = lax.dot_general(
        weights, k_buf[r, :LATENT, :], (((1,), (1,)), ((), ())), preferred_element_type=jnp.float32
    )
    for t in range(TILES):
        out[pl.ds(t * rows + r, pairs, stride=rows * TILES + 1), :] = numerators[
            :, t * LANES : (t + 1) * LANES
        ]


def finish(out, s_buf, k_buf, odd_wanted):
    rows = k_buf.shape[0]
    pairs = s_buf.shape[2] // 2
    stats = jnp.zeros((pairs, LANES), jnp.float32)
    weights = []
    for r in range(rows):
        exponent, stats = soften(s_buf, r, odd_wanted, stats)
        weights.append(exponent)
    for r in range(rows):
        weigh(out, weights[r], k_buf, r)
    out[pl.ds(rows * TILES, pairs, stride=rows * TILES + 1), :] = stats


def attend_theirs(lengths, queries, cache, theirs, s_buf, k_buf, l_buf, q_buf, arrived):
    rows, heads, _ = queries.shape
    shard_len = cache.shape[2]
    me = lax.axis_index("kv")
    first_core = lax.rem(me, 2) == 0
    small = [
        pltpu.make_async_copy(lengths, l_buf, arrived.at[rows]),
        pltpu.make_async_copy(queries, q_buf, arrived.at[rows + 1]),
    ]
    large = [pltpu.make_async_copy(cache.at[r], k_buf.at[r], arrived.at[r]) for r in range(rows)]
    for copy in small + large:
        copy.start()
    position = me * shard_len + lax.broadcasted_iota(jnp.int32, (1, shard_len), 1)
    stats = [jnp.zeros((heads // 2, LANES), jnp.float32)]
    weights = {}

    def score(r):
        scores = jnp.dot(q_buf[r], k_buf[r], preferred_element_type=jnp.float32) * softmax_scale
        scores = jnp.where(position < l_buf[r], scores, masked_value)
        for t in range(shard_len // LANES):
            s_buf[r, t] = scores[:, t * LANES : (t + 1) * LANES]

    def exponents(r):
        weights[r], stats[0] = soften(s_buf, r, first_core, stats[0])

    def numerators(r):
        weigh(theirs, weights[r], k_buf, r)

    for copy in small:
        copy.wait()
    parts = [range(4), range(4, rows)]
    for step in range(4):
        if step < 2:
            for r in parts[step]:
                large[r].wait()
        for part, stage in ((step - 2, numerators), (step - 1, exponents), (step, score)):
            if 0 <= part < 2:
                for r in parts[part]:
                    stage(r)
    theirs[pl.ds(rows * TILES, heads // 2, stride=rows * TILES + 1), :] = stats[0]


def attend_mine(s_buf, k_buf, mine):
    finish(mine, s_buf, k_buf, lax.rem(lax.axis_index("kv"), 2) == 1)


def merge_cores(rows, order, got, mine, merged):
    sent = rows * TILES + 1
    chips = len(order)
    stats = [ref[pl.ds(rows * TILES, chips, stride=sent), :] for ref in (got, mine)]
    top = jnp.maximum(*stats)
    weights = [jnp.exp(s - top) for s in stats]
    total = sum(pltpu.roll(s, HALF, 1) * w for s, w in zip(stats, weights))
    both = jnp.where(lane_of(chips) < HALF, top, pltpu.roll(total, HALF, 1))
    columns = [jnp.transpose(w)[:rows] for w in weights]
    turned = jnp.concatenate([both[order[0] :], both[: order[0]]], axis=0)
    merged[pl.ds(rows * TILES, chips, stride=sent), :] = turned
    for slot, q in enumerate(order):
        factors = [jnp.broadcast_to(c[:, q : q + 1], (rows, LANES)) for c in columns]
        for t in range(TILES):
            at = pl.ds(q * sent + t * rows, rows)
            merged[slot * sent + t * rows : slot * sent + (t + 1) * rows, :] = (
                got[at, :] * factors[0] + mine[at, :] * factors[1]
            )


def project(rows, order, got, value_up, out_proj, theirs, mine):
    sent = rows * TILES + 1
    chips = got.shape[0] // sent
    features = out_proj.shape[1] // (2 * chips)
    core = lax.rem(lax.axis_index("kv"), 2)
    stats = got[pl.ds(TILES * rows, chips, stride=sent), :]
    weight = jnp.exp(stats - jnp.max(stats, axis=0, keepdims=True))
    total = jnp.sum(weight * pltpu.roll(stats, HALF, 1), axis=0, keepdims=True)
    total = jnp.transpose(jnp.broadcast_to(total, (rows, LANES)))[:rows, :1]
    combined = [
        jnp.concatenate(
            [
                jnp.sum(
                    got[pl.ds(t * rows + r, chips, stride=sent), :] * weight[:, r : r + 1],
                    axis=0,
                    keepdims=True,
                )
                for r in range(rows)
            ],
            axis=0,
        )
        for t in range(TILES)
    ]
    head_values = jnp.dot(
        jnp.concatenate(combined, axis=1).astype(jnp.bfloat16),
        value_up[0],
        preferred_element_type=jnp.float32,
    )
    projection = jnp.dot(
        (head_values / total).astype(jnp.bfloat16), out_proj[...], preferred_element_type=jnp.float32
    )
    spare = LANES - features
    lane = lane_of(rows)
    pad = jnp.zeros((rows, spare), jnp.float32)
    for slot, q in enumerate(order):
        blocks = []
        for d in (2 * q, 2 * q + 1):
            part = jnp.concatenate([projection[:, d * features : (d + 1) * features], pad], axis=1)
            last = jnp.broadcast_to(part[rows - 1 :], (rows, LANES))
            last = pltpu.roll(last, spare, 1, stride=spare, stride_axis=0)
            blocks.append(jnp.where(lane < features, part, last))
        at = pl.ds(slot * (rows - 1), rows - 1)
        theirs[at, :] = jnp.where(core == 0, blocks[1], blocks[0])[: rows - 1]
        mine[at, :] = jnp.where(core == 0, blocks[0], blocks[1])[: rows - 1]


def add_other(both, mine, out):
    at = pl.ds(0, out.shape[0])
    out[...] = mine[at, :] + both[1 - lax.rem(lax.axis_index("kv"), 2), at, :]


def add_up(got, out):
    rows, features = out.shape
    spare = LANES - features
    count = got.shape[0]
    parts = [got[pl.ds(j, rows - 1), :] for j in range(0, count - rows + 1, rows - 1)]
    parts.append(got[pl.ds(count - rows, rows), :][1:])
    while len(parts) > 1:
        parts = [sum(parts[i : i + 2]) for i in range(0, len(parts), 2)]
    total = parts[0]
    last = [total[i : i + 1, features:] for i in reversed(range(rows - 1))]
    out[...] = jnp.concatenate(
        [total[:, :features], jnp.concatenate(last, axis=1)], axis=0
    ).astype(out.dtype)


def core_swap(x, kv):
    return lax.ppermute(x, "kv", [(i, i ^ 1) for i in range(kv)])


def chips_from(first, chips):
    return [(first + i) % chips for i in range(chips)]


def on_device(kv, queries, latent_cache, lengths, value_up, out_proj):
    rows, heads, width = queries.shape
    shard_len = latent_cache.shape[1]
    chips = kv // 2
    columns, down = 4, chips // 4
    blocks = [((2 - i) % columns) * down + (3 + j) % down for i in range(columns) for j in range(down)]
    orders = [chips_from(26, chips), blocks]
    same_core = [[[2 * i + c for i in order] for c in range(2)] for order in orders]
    params = pltpu.CompilerParams(vmem_limit_bytes=8 * 2**20)
    f32 = jnp.float32

    sent = rows * TILES + 1
    partials = jax.ShapeDtypeStruct((chips * sent, LANES), f32)
    theirs, scores, held = pl.pallas_call(
        attend_theirs,
        out_shape=[
            partials,
            jax.ShapeDtypeStruct((rows, shard_len // LANES, heads, LANES), f32),
            jax.ShapeDtypeStruct((rows, width, shard_len), latent_cache.dtype),
        ],
        in_specs=[pl.BlockSpec(memory_space=pltpu.HBM)] * 3,
        out_specs=vmem_specs(3),
        scratch_shapes=[
            pltpu.SMEM((rows,), lengths.dtype),
            pltpu.VMEM((rows, heads, width), queries.dtype),
            pltpu.SemaphoreType.DMA((rows + 2,)),
        ],
        compiler_params=params,
    )(*[in_hbm(v) for v in (lengths, queries, latent_cache.transpose(0, 2, 1))])
    got = core_swap(theirs, kv)
    mine = pl.pallas_call(
        attend_mine,
        out_shape=partials,
        in_specs=vmem_specs(2),
        out_specs=vmem_specs(1)[0],
        compiler_params=params,
    )(scores, held)
    merged = pl.pallas_call(
        lambda *refs: merge_cores(rows, orders[0], *refs),
        out_shape=partials,
        in_specs=vmem_specs(2),
        out_specs=vmem_specs(1)[0],
        compiler_params=params,
    )(got, mine)
    got = lax.all_to_all(
        merged.reshape(chips, 1, sent * LANES), "kv", 0, 0, axis_index_groups=same_core[0]
    ).reshape(chips * sent, LANES)
    packed = jax.ShapeDtypeStruct((chips * (rows - 1), LANES), f32)
    features = jax.ShapeDtypeStruct((chips * (rows - 1) + rows, LANES), f32)
    theirs, mine = pl.pallas_call(
        lambda *refs: project(rows, orders[1], *refs),
        out_shape=[features] * 2,
        in_specs=vmem_specs(3),
        out_specs=vmem_specs(2),
        compiler_params=params,
    )(got, value_up, out_proj)
    both = lax.all_gather(
        theirs, "kv", axis_index_groups=[[2 * i, 2 * i + 1] for i in range(chips)]
    )
    summed = pl.pallas_call(
        add_other,
        out_shape=packed,
        in_specs=vmem_specs(2),
        out_specs=vmem_specs(1)[0],
        compiler_params=params,
    )(both, mine)
    parts = lax.all_to_all(
        summed.reshape(chips, 1, (rows - 1) * LANES), "kv", 0, 0, axis_index_groups=same_core[1]
    ).reshape(chips * (rows - 1), LANES)
    return pl.pallas_call(
        add_up,
        out_shape=jax.ShapeDtypeStruct((rows, out_proj.shape[1] // kv), jnp.bfloat16),
        in_specs=vmem_specs(1),
        compiler_params=params,
    )(parts)


def solution(mesh):
    kv = mesh.shape["kv"]
    placed = (
        P("rep", None, None),
        P("rep", "kv", None),
        P("rep"),
        P("kv", None, None),
        P("kv", None),
    )

    def device_step(*args):
        return on_device(kv, *args)

    return jax.shard_map(
        device_step, mesh=mesh, in_specs=placed, out_specs=P("rep", "kv"), check_vma=False
    )
```
